256 devices in a mesh: ty: 8 (over z_hi, x), tx: 16 (over z_lo, y), ens: 2 (over core).
Axes of the slice: x: 4, y: 4, z: 8 (z_hi: 2, z_lo: 4; z = z_hi * 4 + z_lo), core: 2. Of those that a mesh axis runs over, the one named last changes fastest.
Arguments:
- anomalies: float32 [4, 8, 1024, 2048], P('ens', None, 'ty', 'tx'), may hold values from -6 to 6
- climate_variance: float32 [8, 1024, 2048], P(None, 'ty', 'tx'), may hold values from 0.05 to 2
Outputs:
- covaried: float32 [4, 8, 1024, 2048], P('ens', None, 'ty', 'tx')
The draws below stay inside these ranges and needn't reach their ends.
All inputs are finite; a program needn't handle non-finite values.
Results may differ from the reference program's by a relative error of at most 0.0001.
Values sent between devices are 32-bit elements; how exact they have to be, the bound alone decides.
No kernel may reach another device: no remote copies, remote signals or barrier semaphores. Data moves between devices by JAX's collectives and lax.ppermute only.
A program may use at most 64 MiB of HBM per device.

```python
import math
import jax
import jax.numpy as jnp
from jax import lax

VLEV = 8
LEVELS = 5
NY = 1024
NX = 2048
MEMBERS = 4


def shard_levels(own_key, dims, split, smallest, largest):
    level, own = 1.0, jax.random.fold_in(own_key, 6)
    for axis_at, parts in split:
        draws = jnp.exp(jax.random.uniform(jax.random.fold_in(own, axis_at), (parts,), jnp.float32, smallest / len(split), largest / len(split)))
        level = level * jnp.repeat(draws, dims[axis_at] // parts).reshape([-1 if axis == axis_at else 1 for axis in range(len(dims))])
    return level


def normal_values(key, dims, spread, reach, cuts=(), held_as=jnp.bfloat16):
    drawn = jax.random.normal(key, dims, jnp.float32) * spread
    if len(cuts) > 0:
        drawn = shard_levels(key, dims, cuts, -0.22, 0.18) * drawn
    return jnp.clip(drawn, min=-reach, max=reach).astype(held_as)


def setup_inputs(seed: int = 0) -> dict:
    streams_of = jax.random.split(jax.random.key(seed), 3)
    return {
        "anomalies": normal_values(streams_of[0], (MEMBERS, VLEV, NY, NX), 1.0, 6.0, ((0, 2), (2, 8), (3, 16)), jnp.float32),
        "climate_variance": jnp.clip(jnp.exp(math.log(2.0) - 3.6888794 * jax.random.uniform(streams_of[1], (VLEV, NY, NX), jnp.float32) ** shard_levels(streams_of[1], (VLEV, NY, NX), ((1, 8), (2, 16)), -0.2, 0.2)), 0.05, 2.0),
    }


root_three = math.sqrt(3.0)
norm_factor = 4.0 * math.sqrt(2.0)
low_taps = ((1.0 + root_three) / norm_factor, (3.0 + root_three) / norm_factor, (3.0 - root_three) / norm_factor, (1.0 - root_three) / norm_factor)
high_taps = (low_taps[3], -low_taps[2], low_taps[1], -low_taps[0])

def analyse_axis(values, along_axis):
    length = values.shape[along_axis]
    even_cells = lax.slice_in_dim(values, 0, length, 2, along_axis)
    odd_cells = lax.slice_in_dim(values, 1, length, 2, along_axis)
    next_even = jnp.roll(even_cells, -1, along_axis)
    next_odd = jnp.roll(odd_cells, -1, along_axis)
    lowpass = low_taps[0] * even_cells + low_taps[1] * odd_cells + low_taps[2] * next_even + low_taps[3] * next_odd
    highpass = high_taps[0] * even_cells + high_taps[1] * odd_cells + high_taps[2] * next_even + high_taps[3] * next_odd
    return (lowpass, highpass)

def alternate(even_part, odd_part, along_axis):
    stacked = jnp.stack([even_part, odd_part], along_axis + 1)
    target = list(even_part.shape)
    target[along_axis] = target[along_axis] * 2
    return stacked.reshape(target)

def synthesise_axis(lowpass, highpass, along_axis):
    prior_low = jnp.roll(lowpass, 1, along_axis)
    prior_high = jnp.roll(highpass, 1, along_axis)
    even_part = low_taps[0] * lowpass + high_taps[0] * highpass + low_taps[2] * prior_low + high_taps[2] * prior_high
    odd_part = low_taps[1] * lowpass + high_taps[1] * highpass + low_taps[3] * prior_low + high_taps[3] * prior_high
    return alternate(even_part, odd_part, along_axis)

def blended(coefficient, climate_part):
    ensemble_part = lax.optimization_barrier(jnp.sum(coefficient * coefficient, axis=0)) / MEMBERS
    return coefficient * (0.5 * climate_part + 0.5 * ensemble_part)[None]

def apply_level(inputs):
    members_field, climate = inputs
    approx = members_field
    details = []
    for level_index in range(LEVELS):
        col_low, col_high = analyse_axis(approx, 2)
        low_low, high_low = analyse_axis(col_low, 1)
        low_high, high_high = analyse_axis(col_high, 1)
        details.append((low_high, high_low, high_high))
        approx = low_low
    scaled_details = []
    for level_index in range(LEVELS):
        stride = 2 ** level_index
        period = 2 * stride
        low_high, high_low, high_high = details[level_index]
        scaled_details.append((blended(low_high, climate[0::period, stride::period]), blended(high_low, climate[stride::period, 0::period]), blended(high_high, climate[stride::period, stride::period])))
    coarsest = 2 ** LEVELS
    approx = blended(approx, climate[0::coarsest, 0::coarsest])
    for level_index in reversed(range(LEVELS)):
        low_high, high_low, high_high = scaled_details[level_index]
        col_low = synthesise_axis(approx, high_low, 1)
        col_high = synthesise_axis(low_high, high_high, 1)
        approx = synthesise_axis(col_low, col_high, 2)
    return approx

def reference(anomalies, climate_variance):
    by_level = jnp.moveaxis(anomalies, 1, 0)
    result = lax.map(apply_level, (by_level, climate_variance))
    return jnp.moveaxis(result, 0, 1)
```

```python
import functools
import math

import jax
import jax.numpy as jnp
import ml_dtypes
import numpy as np
from jax import lax
from jax.experimental import pallas as pl
from jax.experimental.pallas import tpu as pltpu
from jax.sharding import PartitionSpec as P

LEVELS = 5
N = 128
EXT = 24

root_three = math.sqrt(3.0)
norm_factor = 4.0 * math.sqrt(2.0)
low_taps = np.array([1.0 + root_three, 3.0 + root_three, 3.0 - root_three, 1.0 - root_three]) / norm_factor
high_taps = np.array([low_taps[3], -low_taps[2], low_taps[1], -low_taps[0]])


def express(rows, basis):
    solved = np.linalg.lstsq(basis.T, rows.T, rcond=1e-9)[0].T
    assert np.abs(solved @ basis - rows).max() < 1e-10
    return solved


def build():
    approx = np.zeros((N + 2, N))
    approx[2:] = np.eye(N)
    A = np.zeros((256, N))
    PM = np.zeros((256, N))
    level = np.zeros(256, int)
    is_low = np.zeros(256, bool)
    valid = np.zeros(256, bool)
    E = np.zeros((EXT, N))
    last = np.zeros((EXT, N))
    last_pm = np.zeros((EXT, N))
    ext_level = np.full(EXT, -1)
    ext_low = np.zeros(EXT, bool)
    S = np.zeros((LEVELS, N))
    T = []
    up = np.zeros((LEVELS, 3, N))
    down = np.zeros((LEVELS, 3, N))
    up_k = np.zeros((LEVELS, 4, 3))
    down_k = np.zeros((LEVELS, 4, 3))
    where_last = np.zeros((LEVELS, 4), int)
    offset, count = 0, N
    for l in range(LEVELS):
        half = count // 2
        bands = []
        for taps in (low_taps, high_taps):
            band = np.zeros((half + 2, N))
            for k in range(-2, half):
                for j in range(4):
                    if -2 <= 2 * k + j < count:
                        band[k + 2] += taps[j] * approx[2 * k + j + 2]
            bands.append(band)
        stride = 2**l
        for b, band in enumerate(bands):
            width = max(half, 8)
            start = offset + width - half
            A[start : start + half] = band[2:]
            valid[start : start + half] = True
            level[offset : offset + width] = l
            is_low[offset : offset + width] = b == 0
            for k in range(half):
                PM[start + k, 2 * stride * k + (0 if b == 0 else stride)] = 1.0
            for k in range(2):
                e = 4 * l + 2 * b + k
                where_last[l, 2 * b + k] = start + half - 2 + k
                ext_level[e], ext_low[e] = l, b == 0
                if l > 0 or k == 1:
                    E[e] = band[k]
                    last[e] = A[start + half - 2 + k]
                    last_pm[e] = PM[start + half - 2 + k]
                else:
                    ext_level[e] = -1
            offset += width
        S[l] = low_taps[2] * approx[2] + low_taps[3] * approx[3]
        t = low_taps[0] * approx[count] + low_taps[1] * approx[count + 1]
        if l == 0:
            T.append(t)
            up[0, 0], down[0, 0] = S[0], t
        else:
            if l == 1:
                T.append(t)
            T += [bands[0][half], bands[1][half]]
            up[l] = np.stack([approx[0], approx[1], S[l]])
            down[l] = np.stack([t, bands[0][half], bands[1][half]])
        up_k[l] = express(E[4 * l : 4 * l + 4], up[l])
        down_k[l] = express(last[4 * l : 4 * l + 4], down[l])
        approx, count = bands[0], half
    T = np.stack(T)
    same = (level[:, None] == level[None, :]) & valid[:, None] & valid[None, :]
    mask = same & ~(is_low[:, None] & is_low[None, :] & (level[:, None] < 4))
    c = {}
    c["A"], c["PM"] = A, PM
    c["E"] = E
    c["S"], c["T"] = S, T
    c["KE"], c["KA"] = express(E, S), express(last, T)
    place = np.zeros((256, EXT))
    for l in range(LEVELS):
        for q in range(4):
            place[where_last[l, q], 4 * l + q] = 1.0
    c["GS"] = (place @ c["KE"]).T
    columns = sorted({int(np.argmax(r)) for r in last_pm if r.any()})
    D = np.zeros((12, N))
    for i, col in enumerate(columns):
        D[i, col] = 1.0
    c["D"] = D
    c["KD"] = last_pm @ D.T
    Y = np.zeros((LEVELS, 8, N))
    PY = np.zeros((LEVELS, 8, N))
    PYC = np.zeros((LEVELS, 8, N))
    for l in range(LEVELS):
        if l == 0:
            Y[0, 3], Y[0, 7] = up[0, 0], down[0, 0]
            PY[0, 4:8] = last_pm[0:4]
        else:
            Y[l, 0:3], Y[l, 4:7] = up[l], down[l]
            PY[l, 0:4] = last_pm[4 * l : 4 * l + 4]
        PYC[l, 0:4] = last_pm[4 * l : 4 * l + 4]
    c["Y"], c["PY"], c["PYC"] = Y.reshape(40, N), PY.reshape(40, N), PYC.reshape(40, N)
    GK = np.zeros((256, 4))
    cup = np.zeros((4, 8, N))
    cdn = np.zeros((4, 8, N))
    hup = np.zeros((4, 8, 96))
    hdn = np.zeros((4, 8, 96))
    lane_level = level[128:]
    ext96 = np.tile(ext_level, 4)
    for l in range(LEVELS):
        for q in range(4):
            for j in range(3):
                row = 3 if l == 0 else j
                if l == 0 and j > 0:
                    continue
                GK[where_last[l, q], row] = up_k[l, q, j]
                if l == 0:
                    cup[3, 4 + q, :] = up_k[0, q, 0]
                    cdn[3, 4 + q, :] = down_k[0, q, 0]
                else:
                    cup[j, q, lane_level == l] = up_k[l, q, j]
                    cdn[j, q, lane_level == l] = down_k[l, q, j]
                hup[row, q, ext96 == l] = up_k[l, q, j]
                hdn[row, q, ext96 == l] = down_k[l, q, j]
    c["GK"] = GK
    c["cup"], c["cdn"], c["hup"], c["hdn"] = cup, cdn, hup, hdn
    c["m0"], c["m1"] = mask[:128, :128], mask[128:, 128:]
    ext_mask = (ext_level[:, None] == level[None, :]) & valid[None, :]
    ext_mask &= ~(ext_low[:, None] & is_low[None, :] & (level[None, :] < 4))
    c["mlh"] = ext_mask
    mth = np.zeros((8, N), bool)
    for q in range(4):
        low = q < 2
        mth[q] = valid[128:] & ~(low & is_low[128:] & (lane_level < 4))
        if q % 2 == 1:
            mth[4 + q] = ~(low & is_low[:128])
    c["mth"] = mth
    mch = np.zeros((8, EXT), bool)
    for q in range(4):
        low = q < 2
        mch[q] = (ext_level >= 0) & ~(low & ext_low & (ext_level < 4))
        mch[q] &= ~((ext_level == 0) & (q % 2 == 0))
    c["mch"] = np.tile(mch, (1, 4))
    c["lane_level"], c["ext_level"] = lane_level, ext_level
    return c


def three(matrix, axis, reverse=False):
    high = matrix.astype(ml_dtypes.bfloat16)
    low = (matrix - high.astype(np.float64)).astype(ml_dtypes.bfloat16)
    return np.concatenate([high, high, low], axis)


def pad_rows(matrix, rows):
    return np.concatenate([matrix, np.zeros((rows - matrix.shape[0], matrix.shape[1]))], 0)


def pad_cols(matrix, cols):
    return pad_rows(matrix.T, cols).T


@functools.cache
def constants():
    c = build()
    f32 = np.float32
    k = {}
    k["q_nt"] = three(np.concatenate([pad_rows(c["T"], 16), pad_rows(c["S"], 16)]), 1)
    k["d_nt"] = np.concatenate([pad_rows(c["D"], 16)] * 2, 1).astype(ml_dtypes.bfloat16)
    k["at"] = three(c["A"].T, 0)
    k["gs"] = three(pad_rows(c["GS"], 16), 0)
    k["e_nt"] = three(pad_rows(c["E"], 32), 1)
    k["ka"] = three(pad_rows(pad_cols(c["KA"], 16), 32), 1)
    k["kd"] = np.concatenate([pad_rows(pad_cols(c["KD"], 16), 32)] * 2, 1).astype(ml_dtypes.bfloat16)
    k["y0"] = three(pad_rows(c["Y"][:8], 16), 1)
    k["y1"] = three(c["Y"][8:], 1)
    k["y_nt"] = three(pad_rows(c["Y"], 48), 1)
    k["pt"] = np.concatenate([c["PM"].T] * 2, 0).astype(ml_dtypes.bfloat16)
    k["p0"] = np.concatenate([c["PM"][:128]] * 2, 1).astype(ml_dtypes.bfloat16)
    k["p1"] = np.concatenate([c["PM"][128:]] * 2, 1).astype(ml_dtypes.bfloat16)
    k["py0"] = np.concatenate([pad_rows(c["PY"][:8], 16)] * 2, 1).astype(ml_dtypes.bfloat16)
    k["py1"] = np.concatenate([c["PY"][8:]] * 2, 1).astype(ml_dtypes.bfloat16)
    k["pyc_nt"] = np.concatenate([pad_rows(c["PYC"], 48)] * 2, 1).astype(ml_dtypes.bfloat16)
    gk = pad_cols(c["GK"], 16)
    k["a0"] = np.concatenate([three(c["A"][:128], 1), three(gk[:128], 1)], 1)
    k["a1"] = np.concatenate([three(c["A"][128:], 1), three(gk[128:], 1)], 1)
    k["gkt"] = three(gk.T, 0)
    k["s0"] = three(c["A"][:128], 0)
    k["s1"] = three(c["A"][128:], 0)
    k["e_tn"] = three(pad_rows(c["E"], 32), 0)
    k["e4"] = three(np.concatenate([c["E"]] * 4), 0)
    ey = np.zeros((40, N))
    ey[4:8] = c["E"][0:4]
    for l in range(1, LEVELS):
        ey[8 * l : 8 * l + 4] = c["E"][4 * l : 4 * l + 4]
    k["o"] = three(np.concatenate([c["A"].T, ey.T, np.zeros((N, 24))], 1), 1)
    for name in ("cup", "cdn", "hup", "hdn"):
        k[name] = c[name].astype(f32)
    lane = c["lane_level"]
    k["fold"] = np.stack([np.broadcast_to(lane == l, (8, N)) for l in range(1, LEVELS)]).astype(f32)
    ext96 = np.tile(c["ext_level"], 4)
    k["foldx"] = np.stack([np.broadcast_to(ext96 == l, (8, 96)) for l in range(LEVELS)]).astype(f32)
    k["m0"], k["m1"] = c["m0"].astype(f32), c["m1"].astype(f32)
    k["mlh"], k["mth"], k["mch"] = c["mlh"].astype(f32), c["mth"].astype(f32), c["mch"].astype(f32)
    tl = np.zeros((LEVELS, 8, N))
    tl[0, 4:8] = 1.0
    for l in range(1, LEVELS):
        tl[l, 0:4, lane == l] = 1.0
    k["tl"] = tl.astype(f32)
    cl = np.zeros((LEVELS, 4, 8, 96))
    image = np.repeat(np.arange(4), EXT)
    for l in range(LEVELS):
        for i in range(4):
            rows = slice(4, 8) if l == 0 else slice(0, 4)
            cl[l, i, rows, (ext96 == l) & (image == i)] = 1.0
    k["cl"] = cl.astype(f32)
    return k


def split(x):
    high = x.astype(jnp.bfloat16).astype(jnp.float32)
    return high, x - high


def data3(x, axis):
    high, low = split(x)
    return jnp.concatenate([high, low, high], axis).astype(jnp.bfloat16)


def data2(x, axis):
    high, low = split(x)
    return jnp.concatenate([high, low], axis).astype(jnp.bfloat16)


def nn(a, b):
    return lax.dot_general(a, b, (((1,), (0,)), ((), ())), preferred_element_type=jnp.float32)


def nt(a, b):
    return lax.dot_general(a, b, (((1,), (1,)), ((), ())), preferred_element_type=jnp.float32)


def tn(a, b):
    return lax.dot_general(a, b, (((0,), (0,)), ((), ())), preferred_element_type=jnp.float32)


def lanes(x, i):
    return x[:, N * i : N * (i + 1)]


def rows(x, i):
    return x[N * i : N * (i + 1)]


def side_by_side(x):
    return jnp.concatenate([rows(x, i) for i in range(4)], 1)


def stacked(x):
    return jnp.concatenate([lanes(x, i) for i in range(4)], 0)


def zeros(*shape):
    return jnp.zeros(shape, jnp.float32)


def first_kernel(x_ref, clim_ref, q_nt, d_nt, a_ref, b_ref):
    even = lax.axis_index("tx") % 2 == 0
    ens = lax.axis_index("ens")
    x3 = data3(x_ref[...].reshape(4 * N, N), 1)
    u = nt(q_nt[...], x3)
    clim = clim_ref[ens]
    d = nt(d_nt[...], data2(clim, 1))
    right = [u[0:10, N * i : N * (i + 1)] for i in range(4)] + [d[0:12], zeros(4, N)]
    left = [u[16:26, N * i : N * (i + 1)] for i in range(4)] + [zeros(16, N)]
    right, left = jnp.concatenate(right, 0), jnp.concatenate(left, 0)
    a_ref[0] = jnp.where(even, right, left)
    b_ref[0] = jnp.where(even, left, right)


def columns_of(x3, from_right, k):
    fr = jnp.concatenate([from_right[10 * i : 10 * i + 5] for i in range(4)], 1)
    fr = jnp.concatenate([fr, zeros(11, 4 * N)], 0)
    return nn(x3, k["at"]) + tn(data3(fr, 0), k["gs"])


def left_columns(x3, from_left, k):
    fl = jnp.concatenate([from_left[10 * i : 10 * i + 10] for i in range(4)], 1)
    fl = jnp.concatenate([fl, zeros(6, 4 * N)], 0)
    zl = nt(k["e_nt"], x3) + nn(k["ka"], data3(fl, 0))
    return jnp.concatenate([zl[0:EXT, N * i : N * (i + 1)] for i in range(4)], 0)


def left_clim(from_left, k):
    d = jnp.concatenate([from_left[40:52], zeros(4, N)], 0)
    return nn(k["kd"], data2(d, 0))[0:EXT]


SECOND = ("at", "gs", "e_nt", "ka", "kd", "y0", "y1", "y_nt", "pt", "py0", "py1", "pyc_nt", "fold", "foldx")


def second_kernel(x_ref, clim_ref, ra_ref, rb_ref, *refs):
    k = {name: ref[...] for name, ref in zip(SECOND, refs)}
    a_ref, b_ref, up_ref = refs[len(SECOND) :]
    even = lax.axis_index("tx") % 2 == 0
    even_y = lax.axis_index("ty") % 2 == 0
    ens = lax.axis_index("ens")
    ra, rb = ra_ref[0], rb_ref[0]
    from_right, from_left = jnp.where(even, ra, rb), jnp.where(even, rb, ra)
    x3 = data3(x_ref[...].reshape(4 * N, N), 1)
    z = columns_of(x3, from_right, k)
    y0 = nn(k["y0"], data3(side_by_side(z[:, :N]), 0))[0:8]
    y1 = nn(k["y1"], data3(side_by_side(z[:, N:]), 0))
    strips = []
    for i in range(4):
        strip = lanes(y0, i)
        for l in range(4):
            strip = strip + k["fold"][l] * lanes(y1[8 * l : 8 * l + 8], i)
        strips.append(strip)
    zl = left_columns(x3, from_left, k)
    hy = nt(k["y_nt"], data3(zl, 1))
    corner = sum(k["foldx"][l] * hy[8 * l : 8 * l + 8] for l in range(LEVELS))
    clim = clim_ref[ens]
    cz = nn(data2(clim, 1), k["pt"])
    cy = nn(k["py0"], data2(cz[:, :N], 0))[0:8]
    cy1 = nn(k["py1"], data2(cz[:, N:], 0))
    for l in range(4):
        cy = cy + k["fold"][l] * cy1[8 * l : 8 * l + 8]
    cx = nt(k["pyc_nt"], data2(left_clim(from_left, k), 1))
    cc = sum(k["foldx"][l][:, :EXT] * cx[8 * l : 8 * l + 8] for l in range(LEVELS))
    up = [s[0:4] for s in strips] + [jnp.concatenate([corner[0:4], zeros(4, 32)], 1), zeros(12, N)]
    down = [s[4:8] for s in strips] + [jnp.concatenate([corner[4:8], cc[0:4], zeros(4, 8)], 1), zeros(4, N), cy]
    up, down = jnp.concatenate(up, 0), jnp.concatenate(down, 0)
    a_ref[0] = jnp.where(even_y, down, up)
    b_ref[0] = jnp.where(even_y, up, down)
    up_ref[0] = up


THIRD = (
    "at", "gs", "e_nt", "ka", "kd", "pt", "p0", "p1", "a0", "a1", "gkt", "s0", "s1", "e_tn", "e4",
    "o", "cup", "cdn", "hup", "hdn", "m0", "m1", "mlh", "mth", "mch", "tl", "cl",
)


def third_kernel(x_ref, xp_ref, clim_ref, ra_ref, rb_ref, rap_ref, rbp_ref, sa_ref, sb_ref, sap_ref, sbp_ref, up_ref, upp_ref, *refs):
    k = {name: ref[...] for name, ref in zip(THIRD, refs)}
    out_ref = refs[len(THIRD)]
    even = lax.axis_index("tx") % 2 == 0
    even_y = lax.axis_index("ty") % 2 == 0
    first = lax.axis_index("ens") == 0
    sides = []
    for x, ra, rb, sa, sb, up in (
        (x_ref, ra_ref, rb_ref, sa_ref, sb_ref, up_ref),
        (xp_ref, rap_ref, rbp_ref, sap_ref, sbp_ref, upp_ref),
    ):
        ra, rb, sa, sb, up = ra[0], rb[0], sa[0], sb[0], up[0]
        from_right, from_left = jnp.where(even, ra, rb), jnp.where(even, rb, ra)
        below, above = jnp.where(even_y, sa, sb), jnp.where(even_y, sb, sa)
        x3 = data3(x[...].reshape(4 * N, N), 1)
        z = columns_of(x3, from_right, k)
        u = jnp.concatenate([below[4 * i : 4 * i + 4] for i in range(4)], 1)
        u3 = data3(jnp.concatenate([u, zeros(12, 4 * N)], 0), 0)
        w0 = nn(k["a0"], jnp.concatenate([data3(side_by_side(z[:, :N]), 0), u3], 0))
        w1 = nn(k["a1"], jnp.concatenate([data3(side_by_side(z[:, N:]), 0), u3], 0))
        zl = left_columns(x3, from_left, k)
        hb = jnp.concatenate([below[16:20, 0:96], zeros(12, 96)], 0)
        lh = nn(data3(zl, 1), k["at"]) + tn(data3(hb, 0), k["gkt"])
        th = []
        for i in range(4):
            t = zeros(8, N)
            for j in range(4):
                t = t + k["cup"][j] * up[4 * i + j : 4 * i + j + 1] + k["cdn"][j] * above[4 * i + j : 4 * i + j + 1]
            th.append(t)
        ch = zeros(8, 96)
        for j in range(4):
            ch = ch + k["hup"][j] * up[16 + j : 17 + j, 0:96] + k["hdn"][j] * above[16 + j : 17 + j, 0:96]
        sides.append((w0, w1, lh, th, ch, from_left, above))
    own, other = sides
    cz = nn(data2(clim_ref[...].reshape(2 * N, N), 1), k["pt"])
    cz0 = jnp.concatenate([cz[:N, :N], cz[N:, :N]], 1)
    cz1 = jnp.concatenate([cz[:N, N:], cz[N:, N:]], 1)
    cw0 = nn(k["p0"], data2(cz0, 0))
    cw1 = nn(k["p1"], data2(cz1, 0))
    halo_left = [jnp.where(first, own[5], other[5]), jnp.where(first, other[5], own[5])]
    halo_above = [jnp.where(first, own[6], other[6]), jnp.where(first, other[6], own[6])]
    s0, s1, slh, sth = [None] * 4, [None] * 4, [None] * 4, [None] * 4
    vch = []
    for v in range(2):
        def variance(clim, mask, parts):
            total = parts[0] * parts[0]
            for part in parts[1:]:
                total = total + part * part
            return mask * (0.5 * clim + 0.125 * total)

        images = (v, v + 2)
        sides4 = [(side, i) for side in (own, other) for i in images]
        v0 = variance(lanes(cw0, v), k["m0"], [lanes(s[0], i) for s, i in sides4])
        v1 = variance(lanes(cw1, v), k["m1"], [lanes(s[1], i) for s, i in sides4])
        clh = nn(data2(left_clim(halo_left[v], k), 1), k["pt"])
        vlh = variance(clh, k["mlh"], [s[2][EXT * i : EXT * (i + 1)] for s, i in sides4])
        vth = variance(halo_above[v][24:32], k["mth"], [s[3][i] for s, i in sides4])
        cch = jnp.concatenate([halo_above[v][16:20, 96:120], zeros(4, EXT)], 0)
        vch.append(variance(cch, k["mch"][:, :EXT], [s[4][:, EXT * i : EXT * (i + 1)] for s, i in sides4]))
        for i in images:
            s0[i] = lanes(own[0], i) * v0
            s1[i] = lanes(own[1], i) * v1
            slh[i] = own[2][EXT * i : EXT * (i + 1)] * vlh
            sth[i] = own[3][i] * vth
    sch = own[4] * jnp.concatenate(vch + vch, 1)
    sch = jnp.concatenate([sch[0:4], sch[0:4]], 0)
    r0 = nn(data3(jnp.concatenate(s0, 0), 1), k["s0"])
    r1 = nn(data3(jnp.concatenate(s1, 0), 1), k["s1"])
    top0 = jnp.concatenate([k["tl"][0] * sth[i] for i in range(4)], 0)
    top1 = jnp.concatenate([k["tl"][l] * sth[i] for l in range(1, LEVELS) for i in range(4)], 0)
    corner = jnp.concatenate([k["cl"][l, i] * sch for l in range(LEVELS) for i in range(4)], 0)
    tu = jnp.concatenate([nn(data3(top0, 1), k["s0"]), nn(data3(top1, 1), k["s1"])], 0)
    tu = tu + nn(data3(corner, 1), k["e4"])
    full = []
    for i in range(4):
        r = tn(data3(jnp.concatenate([slh[i], zeros(8, 256)], 0), 0), k["e_tn"])
        t = jnp.concatenate([tu[8 * (4 * l + i) : 8 * (4 * l + i) + 8] for l in range(LEVELS)] + [zeros(24, N)], 0)
        full.append(jnp.concatenate([r[:N] + rows(r0, i), r[N:] + rows(r1, i), t], 0))
    out = nn(k["o"], data3(jnp.concatenate(full, 1), 0))
    for i in range(4):
        out_ref[i // 2, i % 2] = lanes(out, i)


def whole(array):
    zero = (0,) * array.ndim
    return pl.BlockSpec(array.shape, lambda p: zero)


def block(*shape):
    return pl.BlockSpec((1,) + shape, lambda p: (p, 0, 0))


def call(kernel, names, arguments, in_specs, out_specs, out_shape):
    consts = [jnp.asarray(constants()[name]) for name in names]
    return pl.pallas_call(
        kernel,
        grid=(4,),
        in_specs=in_specs + [whole(c) for c in consts],
        out_specs=out_specs,
        out_shape=out_shape,
        compiler_params=pltpu.CompilerParams(vmem_limit_bytes=48 * 1024 * 1024),
    )(*arguments, *consts)


def exchange(value, axis, odd):
    count = lax.axis_size(axis)
    pairs = [(i, (i + 1 if i % 2 == odd else i - 1) % count) for i in range(count)]
    return lax.ppermute(value, axis, pairs)


def partner(value):
    return lax.ppermute(value, "ens", [(0, 1), (1, 0)])


X_SPEC = pl.BlockSpec((2, 2, N, N), lambda p: (0, p, 0, 0))
CLIM_SPEC = pl.BlockSpec((2, N, N), lambda p: (p, 0, 0))


def shards(x, clim):
    xp = partner(x)
    m1 = jax.ShapeDtypeStruct((4, 56, N), jnp.float32)
    m2 = jax.ShapeDtypeStruct((4, 32, N), jnp.float32)
    b1, b2 = block(56, N), block(32, N)
    xa, xb = call(first_kernel, ("q_nt", "d_nt"), (x, clim), [X_SPEC, CLIM_SPEC], [b1, b1], [m1, m1])
    ra, rb = exchange(xa, "tx", 0), exchange(xb, "tx", 1)
    rap, rbp = partner(ra), partner(rb)
    ya, yb, up = call(second_kernel, SECOND, (x, clim, ra, rb), [X_SPEC, CLIM_SPEC, b1, b1], [b2, b2, b2], [m2, m2, m2])
    sa, sb = exchange(ya, "ty", 0), exchange(yb, "ty", 1)
    upp = partner(up)
    sap, sbp = partner(sa), partner(sb)
    return call(
        third_kernel,
        THIRD,
        (x, xp, clim, ra, rb, rap, rbp, sa, sb, sap, sbp, up, upp),
        [X_SPEC, X_SPEC, CLIM_SPEC] + [b1] * 4 + [b2] * 6,
        X_SPEC,
        jax.ShapeDtypeStruct(x.shape, jnp.float32),
    )


def solution(mesh):
    in_specs = (P("ens", None, "ty", "tx"), P(None, "ty", "tx"))
    out_specs = P("ens", None, "ty", "tx")
    return jax.shard_map(shards, mesh=mesh, in_specs=in_specs, out_specs=out_specs, check_vma=False)
```

```python
import functools
import math

import jax
import jax.numpy as jnp
import ml_dtypes
import numpy as np
from jax import lax
from jax.experimental import pallas as pl
from jax.experimental.pallas import tpu as pltpu
from jax.sharding import PartitionSpec as P

LEVELS = 5
N = 128
EXT = 24

root_three = math.sqrt(3.0)
norm_factor = 4.0 * math.sqrt(2.0)
low_taps = np.array([1.0 + root_three, 3.0 + root_three, 3.0 - root_three, 1.0 - root_three]) / norm_factor
high_taps = np.array([low_taps[3], -low_taps[2], low_taps[1], -low_taps[0]])


def express(rows, basis):
    solved = np.linalg.lstsq(basis.T, rows.T, rcond=1e-9)[0].T
    assert np.abs(solved @ basis - rows).max() < 1e-10
    return solved


def build():
    approx = np.zeros((N + 2, N))
    approx[2:] = np.eye(N)
    A = np.zeros((256, N))
    PM = np.zeros((256, N))
    level = np.zeros(256, int)
    is_low = np.zeros(256, bool)
    valid = np.zeros(256, bool)
    E = np.zeros((EXT, N))
    last = np.zeros((EXT, N))
    last_pm = np.zeros((EXT, N))
    ext_level = np.full(EXT, -1)
    ext_low = np.zeros(EXT, bool)
    S = np.zeros((LEVELS, N))
    T = []
    up = np.zeros((LEVELS, 3, N))
    down = np.zeros((LEVELS, 3, N))
    up_k = np.zeros((LEVELS, 4, 3))
    down_k = np.zeros((LEVELS, 4, 3))
    where_last = np.zeros((LEVELS, 4), int)
    offset, count = 0, N
    for l in range(LEVELS):
        half = count // 2
        bands = []
        for taps in (low_taps, high_taps):
            band = np.zeros((half + 2, N))
            for k in range(-2, half):
                for j in range(4):
                    if -2 <= 2 * k + j < count:
                        band[k + 2] += taps[j] * approx[2 * k + j + 2]
            bands.append(band)
        stride = 2**l
        for b, band in enumerate(bands):
            width = max(half, 8)
            start = offset + width - half
            A[start : start + half] = band[2:]
            valid[start : start + half] = True
            level[offset : offset + width] = l
            is_low[offset : offset + width] = b == 0
            for k in range(half):
                PM[start + k, 2 * stride * k + (0 if b == 0 else stride)] = 1.0
            for k in range(2):
                e = 4 * l + 2 * b + k
                where_last[l, 2 * b + k] = start + half - 2 + k
                ext_level[e], ext_low[e] = l, b == 0
                if l > 0 or k == 1:
                    E[e] = band[k]
                    last[e] = A[start + half - 2 + k]
                    last_pm[e] = PM[start + half - 2 + k]
                else:
                    ext_level[e] = -1
            offset += width
        S[l] = low_taps[2] * approx[2] + low_taps[3] * approx[3]
        t = low_taps[0] * approx[count] + low_taps[1] * approx[count + 1]
        if l == 0:
            T.append(t)
            up[0, 0], down[0, 0] = S[0], t
        else:
            if l == 1:
                T.append(t)
            T += [bands[0][half], bands[1][half]]
            up[l] = np.stack([approx[0], approx[1], S[l]])
            down[l] = np.stack([t, bands[0][half], bands[1][half]])
        up_k[l] = express(E[4 * l : 4 * l + 4], up[l])
        down_k[l] = express(last[4 * l : 4 * l + 4], down[l])
        approx, count = bands[0], half
    T = np.stack(T)
    same = (level[:, None] == level[None, :]) & valid[:, None] & valid[None, :]
    mask = same & ~(is_low[:, None] & is_low[None, :] & (level[:, None] < 4))
    c = {}
    c["A"], c["PM"] = A, PM
    c["E"] = E
    c["S"], c["T"] = S, T
    c["KE"], c["KA"] = express(E, S), express(last, T)
    place = np.zeros((256, EXT))
    for l in range(LEVELS):
        for q in range(4):
            place[where_last[l, q], 4 * l + q] = 1.0
    c["GS"] = (place @ c["KE"]).T
    columns = sorted({int(np.argmax(r)) for r in last_pm if r.any()})
    D = np.zeros((12, N))
    for i, col in enumerate(columns):
        D[i, col] = 1.0
    c["D"] = D
    c["KD"] = last_pm @ D.T
    Y = np.zeros((LEVELS, 8, N))
    PY = np.zeros((LEVELS, 8, N))
    PYC = np.zeros((LEVELS, 8, N))
    for l in range(LEVELS):
        if l == 0:
            Y[0, 3], Y[0, 7] = up[0, 0], down[0, 0]
            PY[0, 4:8] = last_pm[0:4]
        else:
            Y[l, 0:3], Y[l, 4:7] = up[l], down[l]
            PY[l, 0:4] = last_pm[4 * l : 4 * l + 4]
        PYC[l, 0:4] = last_pm[4 * l : 4 * l + 4]
    c["Y"], c["PY"], c["PYC"] = Y.reshape(40, N), PY.reshape(40, N), PYC.reshape(40, N)
    GK = np.zeros((256, 4))
    cup = np.zeros((4, 8, N))
    cdn = np.zeros((4, 8, N))
    hup = np.zeros((4, 8, 96))
    hdn = np.zeros((4, 8, 96))
    lane_level = level[128:]
    ext96 = np.tile(ext_level, 4)
    for l in range(LEVELS):
        for q in range(4):
            for j in range(3):
                row = 3 if l == 0 else j
                if l == 0 and j > 0:
                    continue
                GK[where_last[l, q], row] = up_k[l, q, j]
                if l == 0:
                    cup[3, 4 + q, :] = up_k[0, q, 0]
                    cdn[3, 4 + q, :] = down_k[0, q, 0]
                else:
                    cup[j, q, lane_level == l] = up_k[l, q, j]
                    cdn[j, q, lane_level == l] = down_k[l, q, j]
                hup[row, q, ext96 == l] = up_k[l, q, j]
                hdn[row, q, ext96 == l] = down_k[l, q, j]
    c["GK"] = GK
    c["cup"], c["cdn"], c["hup"], c["hdn"] = cup, cdn, hup, hdn
    c["m0"], c["m1"] = mask[:128, :128], mask[128:, 128:]
    ext_mask = (ext_level[:, None] == level[None, :]) & valid[None, :]
    ext_mask &= ~(ext_low[:, None] & is_low[None, :] & (level[None, :] < 4))
    c["mlh"] = ext_mask
    mth = np.zeros((8, N), bool)
    for q in range(4):
        low = q < 2
        mth[q] = valid[128:] & ~(low & is_low[128:] & (lane_level < 4))
        if q % 2 == 1:
            mth[4 + q] = ~(low & is_low[:128])
    c["mth"] = mth
    mch = np.zeros((8, EXT), bool)
    for q in range(4):
        low = q < 2
        mch[q] = (ext_level >= 0) & ~(low & ext_low & (ext_level < 4))
        mch[q] &= ~((ext_level == 0) & (q % 2 == 0))
    c["mch"] = np.tile(mch, (1, 4))
    c["lane_level"], c["ext_level"] = lane_level, ext_level
    return c


def pad_rows(matrix, rows):
    return np.concatenate([matrix, np.zeros((rows - matrix.shape[0],) + matrix.shape[1:])], 0)


def pad_cols(matrix, cols):
    return pad_rows(matrix.T, cols).T


IMAGES = 16
HX = IMAGES * EXT
X_ROWS = 208
Y_ROWS = 112


@functools.cache
def constants():
    c = build()
    k = {}

    def parts(name, matrix, axis):
        k[name] = ("parts", axis, matrix)

    def exact(name, matrix, axis):
        k[name] = ("exact", axis, matrix)

    def mask(name, array):
        k[name] = ("mask", None, np.asarray(array, np.float64))

    def plain(name, array):
        k[name] = ("plain", None, np.asarray(array, np.float64))

    parts("q_nt", np.concatenate([pad_rows(c["T"], 16), pad_rows(c["S"], 16)]), 1)
    exact("d_nt", pad_rows(c["D"], 16), 1)
    parts("at", c["A"].T, 0)
    parts("gs", pad_rows(c["GS"], 16), 0)
    fours = np.kron(np.eye(4), np.concatenate([c["KE"], np.zeros((EXT, 5))], 1))
    parts("kz", pad_cols(np.concatenate([np.kron(np.eye(4), c["KA"]), fours], 1), 128), 1)
    exact("kd", pad_cols(np.kron(np.eye(4), c["KD"]), 128), 1)
    parts("y_nt", pad_rows(c["Y"], 48), 1)
    exact("pt", c["PM"].T, 0)
    exact("p0", c["PM"][:128], 1)
    exact("p1", c["PM"][128:], 1)
    exact("py", pad_rows(c["PY"], 48), 1)
    exact("pyc_nt", pad_rows(c["PYC"], 48), 1)
    gst = np.zeros((128, 256))
    for i in range(8):
        gst[10 * i : 10 * i + 5] = c["GS"]
    parts("gst", gst, 0)
    kdb = np.zeros((128, 128))
    for i in range(4):
        kdb[12 * i : 12 * i + 12, EXT * i : EXT * (i + 1)] = c["KD"].T
    exact("kdb", kdb, 0)
    own = np.zeros((8, 8, 128))
    for i in range(8):
        own[i, :, 10 * i : 10 * i + 10] = 1.0
    mask("own", own)
    parts("gkt", pad_cols(c["GK"], 16).T, 0)
    left = np.arange(N) < 64
    w = np.zeros((9, 4, 8, N))
    for j in range(4):
        g = c["GK"][:, j : j + 1]
        w[0, j] = np.where(left, g[152:160], 0)
        w[1, j] = np.where(left, g[184:192], g[56:64])
        w[2, j] = g[120:128]
        for n, start in enumerate((200, 216, 224, 232, 240, 248)):
            w[3 + n, j] = g[start : start + 8]
    assert np.isclose(np.abs(w[..., 0]).sum() + np.abs(c["GK"][56:64]).sum(), np.abs(c["GK"]).sum())
    plain("gkc", w)
    top = np.concatenate([np.where(left[:, None], 0, c["A"][:N]), np.where(left[:, None], c["A"][N:], 0)], 1)
    parts("st", top, 0)
    parts("s0", c["A"][:128], 0)
    parts("s1", c["A"][128:], 0)
    upper = np.where(left, c["m1"][:64], c["m0"][:64])
    mask("mf", np.concatenate([upper, c["m0"][64:]]))
    mask("ml", c["m1"][64:])
    parts("e_tn", pad_rows(c["E"], 32), 0)
    ey = np.zeros((128, N))
    ey[4:8] = c["E"][0:4]
    for l in range(1, LEVELS):
        ey[8 * l : 8 * l + 4] = c["E"][4 * l : 4 * l + 4]
    parts("o", np.concatenate([c["A"].T, ey.T], 1), 1)
    plain("cup", c["cup"])
    plain("cdn", c["cdn"])
    plain("hup", np.tile(c["hup"][:, :, :EXT], (1, 1, IMAGES)))
    plain("hdn", np.tile(c["hdn"][:, :, :EXT], (1, 1, IMAGES)))
    lane = c["lane_level"]
    ext = np.tile(c["ext_level"], IMAGES)
    mask("fold", np.stack([np.broadcast_to(lane == l, (8, N)) for l in range(1, LEVELS)]))
    mask("foldx", np.stack([np.broadcast_to(ext == l, (8, HX)) for l in range(LEVELS)]))
    mask("mlh", c["mlh"])
    mask("mth", c["mth"])
    mask("mch", np.tile(c["mch"][:, :EXT], (1, 8)))
    tl = np.zeros((LEVELS, 8, N))
    tl[0, 4:8] = 1.0
    for l in range(1, LEVELS):
        tl[l, 0:4, lane == l] = 1.0
    mask("tl", tl)
    cl = np.zeros((LEVELS, 8, 3, 32))
    for l in range(LEVELS):
        cl[l, slice(4, 8) if l == 0 else slice(0, 4), :, :EXT] = c["ext_level"] == l
    mask("cl", cl.reshape(LEVELS, 8, 96))
    return k


def pieces(array, tile):
    array = array.reshape((-1,) + array.shape[-2:])
    width = -(-array.shape[2] // N) * N
    height = -(-array.shape[1] // tile) * tile
    full = np.zeros((array.shape[0], height, width))
    full[:, : array.shape[1], : array.shape[2]] = array
    return full.reshape(array.shape[0], height, width // N, N).transpose(0, 2, 1, 3)


@functools.cache
def packed(names):
    narrow, wide, places = [np.zeros((16, N))], [np.zeros((16, N))], {}
    for name in names:
        kind, axis, array = constants()[name]
        into = wide if kind == "plain" else narrow
        blocks = pieces(array, 8 if kind == "plain" else 16)
        places[name] = (kind, axis, sum(g.shape[0] for g in into), blocks.shape, array.shape)
        if kind == "parts":
            high = blocks.astype(ml_dtypes.bfloat16).astype(np.float64)
            into += [high.reshape(-1, N), (blocks - high).reshape(-1, N)]
        else:
            into.append(blocks.reshape(-1, N))
    arrays = [np.concatenate(narrow).astype(ml_dtypes.bfloat16), np.concatenate(wide).astype(np.float32)]
    return arrays, places


def reader(names, refs):
    places = packed(names)[1]

    def read(name, *index):
        kind, axis, start, blocks, shape = places[name]
        ref = refs[1] if kind == "plain" else refs[0]
        count, columns, height, _ = blocks
        at = 0
        for dim, value in zip(shape, index):
            at = at * dim + value
        assert np.prod(shape[: len(index)], dtype=int) == count

        def one(base):
            first = [base + (at * columns + j) * height for j in range(columns)]
            block = jnp.concatenate([ref[f : f + height, :] for f in first], 1)
            return block

        if kind == "parts":
            high, low = one(start), one(start + count * columns * height)
            return jnp.concatenate([high, high, low], axis)
        if kind == "exact":
            return jnp.concatenate([one(start)] * 2, axis)
        return one(start).astype(jnp.float32)[: shape[-2], : shape[-1]]

    return read


def split(x):
    high = x.astype(jnp.bfloat16).astype(jnp.float32)
    return high, x - high


def data3(x, axis):
    high, low = split(x)
    return jnp.concatenate([high, low, high], axis).astype(jnp.bfloat16)


def data2(x, axis):
    high, low = split(x)
    return jnp.concatenate([high, low], axis).astype(jnp.bfloat16)


def nn(a, b):
    return lax.dot_general(a, b, (((1,), (0,)), ((), ())), preferred_element_type=jnp.float32)


def nt(a, b):
    return lax.dot_general(a, b, (((1,), (1,)), ((), ())), preferred_element_type=jnp.float32)


def tn(a, b):
    return lax.dot_general(a, b, (((0,), (0,)), ((), ())), preferred_element_type=jnp.float32)


def lanes(x, i):
    return x[:, N * i : N * (i + 1)]


def rows(x, i):
    return x[N * i : N * (i + 1)]


def side_by_side(x):
    return jnp.concatenate([rows(x, i) for i in range(x.shape[0] // N)], 1)


def zeros(*shape):
    return jnp.zeros(shape, jnp.float32)


def wider(x, width):
    return jnp.concatenate([x, zeros(x.shape[0], width - x.shape[1])], 1)


def taller(x, height):
    return jnp.concatenate([x, zeros(height - x.shape[0], x.shape[1])], 0)


def even_place(axis):
    return lax.axis_index(axis) % 2 == 0


HALF = 64
H = [float(t) for t in low_taps]
G = [float(t) for t in high_taps]


FIRST = ("q_nt", "d_nt")


def first_kernel(x_hbm, clim_hbm, q_hbm, a_ref, b_ref, s_ref, x_ref, clim_ref, q_ref, sems):
    even = even_place("tx")
    ens = lax.axis_index("ens")
    pairs = [(q_hbm, q_ref)]
    for m in range(2):
        for h in range(2):
            pairs.append((x_hbm.at[m, pl.ds(4 * h, 4)], x_ref.at[m, pl.ds(4 * h, 4)]))
    pairs.append((clim_hbm, clim_ref))
    copies = [pltpu.make_async_copy(src, dst, sems.at[i]) for i, (src, dst) in enumerate(pairs)]
    for copy in copies:
        copy.start()
    copies[0].wait()
    k = reader(FIRST, (q_ref,))
    q = k("q_nt")
    right, left = [], []
    for g in range(4):
        copies[1 + g].wait()
        x3 = data3(x_ref[g // 2, 4 * (g % 2) : 4 * (g % 2) + 4].reshape(4 * N, N), 1)
        u = nt(q, x3)
        right += [lanes(u, i)[0:10] for i in range(4)]
        left += [lanes(u, i)[16:26] for i in range(4)]
    copies[5].wait()
    d = nt(k("d_nt"), data2(clim_ref[pl.ds(4 * ens, 4)].reshape(4 * N, N), 1))
    right += [lanes(d, j)[0:12] for j in range(4)]
    left = jnp.concatenate(left, 0)
    s_ref[...] = left
    right, left = jnp.concatenate(right, 0), taller(left, X_ROWS)
    a_ref[...] = jnp.where(even, right, left)
    b_ref[...] = jnp.where(even, left, right)


BESIDE = (
    "at", "fold", "foldx", "gst", "kdb", "kz", "mf", "ml", "own", "p0", "p1", "pt", "py", "pyc_nt",
    "y_nt",
)


def beside_kernel(x_ref, clim_ref, *refs):
    n = 2
    k = reader(BESIDE, refs[:n])
    z_ref, s_ref, c_ref, cf_ref, cl_ref = refs[n:]
    ens = lax.axis_index("ens")
    at = k("at")
    for g in range(4):
        x = x_ref[g // 2, 4 * (g % 2) : 4 * (g % 2) + 4].reshape(4 * N, N)
        z_ref[4 * N * g : 4 * N * (g + 1), :] = nn(data3(x, 1), at)
        y = nn(k("y_nt"), data3(side_by_side(x), 0))
        y = jnp.concatenate([lanes(y, i)[0:40] for i in range(4)], 0)
        y = nn(data3(y, 1), at)
        for i in range(4):
            strip = y[40 * i : 40 * i + 8, :N]
            for l in range(4):
                strip = strip + k("fold", l) * y[40 * i + 8 * l + 8 : 40 * i + 8 * l + 16, N:]
            s_ref[8 * (4 * g + i) : 8 * (4 * g + i) + 8, :] = strip
    clim = clim_ref[pl.ds(4 * ens, 4)].reshape(4 * N, N)
    y = nn(k("py"), data2(side_by_side(clim), 0))
    y = jnp.concatenate([lanes(y, i)[0:40] for i in range(4)], 0)
    y = nn(data2(y, 1), k("pt"))
    for i in range(4):
        strip = y[40 * i : 40 * i + 8, :N]
        for l in range(4):
            strip = strip + k("fold", l) * y[40 * i + 8 * l + 8 : 40 * i + 8 * l + 16, N:]
        c_ref[8 * i : 8 * i + 8, :] = strip
    inside = lax.broadcasted_iota(jnp.int32, (HALF, N), 1) < HALF
    for g in range(2):
        cz = nn(data2(clim_ref[4 * g : 4 * g + 4].reshape(4 * N, N), 1), k("pt"))
        c0 = nn(k("p0"), data2(side_by_side(cz[:, :N]), 0))
        c1 = nn(k("p1"), data2(side_by_side(cz[:, N:]), 0))
        for j in range(4):
            w0, w1 = lanes(c0, j), lanes(c1, j)
            upper = jnp.where(inside, w1[:HALF], w0[:HALF])
            cf_ref[4 * g + j] = 0.5 * k("mf") * jnp.concatenate([upper, w0[HALF:]], 0)
            cl_ref[4 * g + j] = 0.5 * k("ml") * w1[HALF:]


SECOND = (
    "fold", "foldx", "gst", "kdb", "kz", "own", "pyc_nt", "y_nt",
)


def second_kernel(ra_ref, rb_ref, sx_ref, s_ref, c_ref, *refs):
    n = 2
    k = reader(SECOND, refs[:n])
    a_ref, b_ref, up_ref, right_ref, left_ref = refs[n:]
    kz = k("kz")
    even, even_y = even_place("tx"), even_place("ty")
    ra, rb = ra_ref[...], rb_ref[...]
    from_right, from_left = jnp.where(even, ra[:160], rb[:160]), jnp.where(even, rb, ra)
    right_ref[...] = from_right
    strips = []
    for g in range(2):
        f = taller(from_right[80 * g : 80 * g + 80], 128)
        y = nt(k("y_nt"), data3(f, 1))[0:40]
        spread = jnp.concatenate(
            [k("own", i) * y[8 * l : 8 * l + 8] for i in range(8) for l in range(LEVELS)], 0
        )
        t = nn(data3(spread, 1), k("gst"))
        for i in range(8):
            at = 40 * i
            strip = s_ref[64 * g + 8 * i : 64 * g + 8 * i + 8, :] + t[at : at + 8, :N]
            for l in range(4):
                strip = strip + k("fold", l) * t[at + 8 * l + 8 : at + 8 * l + 16, N:]
            strips.append(strip)
    for g in range(4):
        f = jnp.concatenate([from_left[40 * g : 40 * g + 40], sx_ref[40 * g : 40 * g + 40]], 0)
        left_ref[96 * g : 96 * g + 96] = nn(kz, data3(taller(f, 128), 0))
    left_ref[384:432] = from_left[160:208]
    hy = nt(k("y_nt"), data3(left_ref[0:384], 1))
    corner = sum(k("foldx", l) * hy[8 * l : 8 * l + 8] for l in range(LEVELS))
    cx = nt(k("pyc_nt"), data2(taller(from_left[160:208], 128), 1))[0:40]
    cc = nn(data2(cx, 1), k("kdb"))
    cc = sum(k("foldx", l)[:, :N] * cc[8 * l : 8 * l + 8] for l in range(LEVELS))
    up = [s[0:4] for s in strips] + [lanes(corner, g)[0:4] for g in range(3)] + [zeros(36, N)]
    down = [s[4:8] for s in strips] + [lanes(corner, g)[4:8] for g in range(3)] + [cc[0:4], c_ref[...]]
    up, down = jnp.concatenate(up, 0), jnp.concatenate(down, 0)
    a_ref[...] = jnp.where(even_y, down, up)
    b_ref[...] = jnp.where(even_y, up, down)
    up_ref[...] = up


def filtered(ref, count):
    parts = [ref[pl.ds(j, count, stride=2), :] for j in range(4)]
    low = H[0] * parts[0] + H[1] * parts[1] + H[2] * parts[2] + H[3] * parts[3]
    high = G[0] * parts[0] + G[1] * parts[1] + G[2] * parts[2] + G[3] * parts[3]
    return low, high


THIRD = (
    "at", "gs", "kd", "mlh", "pt",
)


def third_kernel(z_ref, xp_ref, fr_ref, fl_ref, frp_ref, flp_ref, *refs):
    n = 2
    k = reader(THIRD, refs[:n])
    wf_ref, wl_ref, lh_ref, clh_ref, order_ref = refs[n : n + 5]
    z0_buf, z1_buf, a_buf, b_buf, c_buf, d_buf = refs[n + 5 :]
    first = lax.axis_index("ens") == 0
    inside = lax.broadcasted_iota(jnp.int32, (HALF, N), 1) < HALF
    at = k("at")
    for side, (fr, fl) in enumerate(((fr_ref, fl_ref), (frp_ref, flp_ref))):
        for g in range(4):
            where = 40 * g
            f = jnp.concatenate([fr[where + 10 * i : where + 10 * i + 5] for i in range(4)], 1)
            z = tn(data3(taller(f, 16), 0), k("gs"))
            if side == 0:
                z = z + z_ref[4 * N * g : 4 * N * (g + 1), :]
            else:
                x = xp_ref[g // 2, 4 * (g % 2) : 4 * (g % 2) + 4].reshape(4 * N, N)
                z = z + nn(data3(x, 1), at)
            zl = fl[96 * g : 96 * g + 96]
            lh_ref[side, 4 * g : 4 * g + 4] = nn(data3(zl, 1), at).reshape(4, EXT, 256)
            for i in range(4):
                image = 4 * g + i
                slot = 16 * side + image
                z0_buf[slot, 0:N] = rows(z, i)[:, :N]
                z1_buf[slot, 0:N] = rows(z, i)[:, N:]
                z0_buf[slot, N : N + 8] = zeros(8, N)
                z1_buf[slot, N : N + 8] = zeros(8, N)
                low0, high0 = filtered(z0_buf.at[slot], 64)
                a_buf[slot, 0:64] = filtered(z1_buf.at[slot], 64)[0]
                a_buf[slot, 64:72] = zeros(8, N)
                low1, high1 = filtered(a_buf.at[slot], 32)
                b_buf[slot, 0:32] = low1
                b_buf[slot, 32:40] = zeros(8, N)
                low2, high2 = filtered(b_buf.at[slot], 16)
                c_buf[slot, 0:16] = low2
                c_buf[slot, 16:24] = zeros(8, N)
                low3, high3 = filtered(c_buf.at[slot], 8)
                d_buf[slot, 0:8] = low3
                d_buf[slot, 8:16] = zeros(8, N)
                low4, high4 = filtered(d_buf.at[slot], 4)
                wf_ref[side, image, 0:64] = jnp.where(inside, jnp.concatenate([low1, high1], 0), low0)
                wf_ref[side, image, 64:128] = high0
                wl_ref[side, image] = jnp.concatenate(
                    [low2, high2, low3, high3, zeros(4, N), low4, zeros(4, N), high4], 0
                )
    mine, other = fl_ref[384:432], flp_ref[384:432]
    halos = [jnp.where(first, mine, other), jnp.where(first, other, mine)]
    for g in range(2):
        cl = nn(k("kd"), data2(taller(halos[g], 128), 0))
        clh = nn(data2(cl, 1), k("pt"))
        for j in range(4):
            clh_ref[4 * g + j] = 0.5 * k("mlh") * clh[EXT * j : EXT * (j + 1)]
    order_ref[...] = zeros(8, N)


def sort_kernel(sa_ref, sb_ref, order_ref, out_ref):
    even_y = even_place("ty")
    a, b = sa_ref[...], sb_ref[...]
    out_ref[0:80] = jnp.where(even_y, a, b)[0:80]
    out_ref[80:192] = jnp.where(even_y, b, a)


FOURTH = (
    "cdn", "cl", "cup", "e_tn", "gkc", "gkt", "hdn", "hup", "mch", "mf", "ml", "mlh", "mth", "o",
    "s0", "s1", "st", "tl",
)


def fourth_kernel(wf_ref, wl_ref, lh_ref, cf_ref, cl_ref, clh_ref, got_ref, gotp_ref, up_ref, upp_ref, *refs):
    n = 2
    k = reader(FOURTH, refs[:n])
    out_ref = refs[n]
    first = lax.axis_index("ens") == 0
    belows, aboves, ups, lhs, chs = [], [], [], [], []
    for got, up in ((got_ref, up_ref), (gotp_ref, upp_ref)):
        below, above, up = got[0:80], got[80:192], up[...]
        hb = jnp.concatenate([below[64 + 4 * g : 68 + 4 * g] for g in range(3)], 1)
        lhs.append(tn(data3(taller(hb, 16), 0), k("gkt")))
        hu = jnp.concatenate([up[64 + 4 * g : 68 + 4 * g] for g in range(3)], 1)
        hd = jnp.concatenate([above[64 + 4 * g : 68 + 4 * g] for g in range(3)], 1)
        ch = zeros(8, HX)
        for j in range(4):
            ch = ch + k("hup", j) * hu[j : j + 1] + k("hdn", j) * hd[j : j + 1]
        belows.append(below)
        aboves.append(above)
        ups.append(up)
        chs.append(ch)
    halos = [jnp.where(first, aboves[0], aboves[1])[76:112], jnp.where(first, aboves[1], aboves[0])[76:112]]

    def top(side, i):
        t = zeros(8, N)
        for j in range(4):
            at = 4 * i + j
            t = t + k("cup", j) * ups[side][at : at + 1] + k("cdn", j) * aboves[side][at : at + 1]
        return t

    def grown(w, side, i, groups):
        parts, done = [], 0
        for start, which, js in groups:
            if start > done:
                parts.append(w[done:start])
            part = w[start : start + 8]
            for j in js:
                part = part + k("gkc", which, j) * belows[side][4 * i + j : 4 * i + j + 1]
            parts.append(part)
            done = start + 8
        return jnp.concatenate(parts + ([w[done:]] if done < w.shape[0] else []), 0)

    def variance(half_clim, mask, parts):
        total = parts[0] * parts[0]
        for part in parts[1:]:
            total = total + part * part
        return half_clim + (0.125 * mask) * total

    in_full = ((24, 0, (0, 1, 2)), (56, 1, (0, 1, 2, 3)), (120, 2, (3,)))
    in_rest = tuple((start, 3 + n, (0, 1, 2)) for n, start in enumerate((8, 24, 32, 40, 48, 56)))
    cch = jnp.concatenate([h[0:4, 0:96] for h in halos], 1)
    cch = jnp.concatenate([cch, zeros(4, 192)], 0)
    vch = variance(0.5 * k("mch") * cch, k("mch"), [c[:, 192 * m : 192 * m + 192] for c in chs for m in range(2)])
    sch = [chs[0][:, 192 * m : 192 * m + 192] * vch for m in range(2)]
    sch = [wider(s, 256) for s in sch]
    edge = []
    for i in range(IMAGES):
        at = EXT * (i % 8)
        c = sch[i // 8][0:4, at : at + EXT]
        edge.append(jnp.concatenate([c, c], 0))
    high, low = split(wider(jnp.concatenate(edge, 0), 32))
    edge = jnp.concatenate([high, low, high], 1)
    edge = jnp.concatenate([k("cl", l) * edge[8 * i : 8 * i + 8] for l in range(LEVELS) for i in range(IMAGES)], 0)
    tu_edge = nn(edge.astype(jnp.bfloat16), k("e_tn"))
    for g in range(4):
        sf, sl, slh, sth = [None] * 4, [None] * 4, [None] * 4, [None] * 4
        for n in range(2):
            v = 2 * g + n
            four = [(side, v + 8 * m) for side in range(2) for m in range(2)]
            wf = [grown(wf_ref[side, i], side, i, in_full) for side, i in four]
            wl = [grown(wl_ref[side, i], side, i, in_rest) for side, i in four]
            lh = [lh_ref[side, i] + lhs[side][EXT * i : EXT * (i + 1)] for side, i in four]
            th = [top(side, i) for side, i in four]
            vf = variance(cf_ref[v], k("mf"), wf)
            vl = variance(cl_ref[v], k("ml"), wl)
            vlh = variance(clh_ref[v], k("mlh"), lh)
            climth = halos[v // 4][4 + 8 * (v % 4) : 12 + 8 * (v % 4)]
            vth = variance(0.5 * k("mth") * climth, k("mth"), th)
            for m in range(2):
                sf[2 * m + n] = wf[m] * vf
                sl[2 * m + n] = wl[m] * vl
                slh[2 * m + n] = lh[m] * vlh
                sth[2 * m + n] = th[m] * vth
        upper = nn(data3(jnp.concatenate([s[:HALF] for s in sf], 0), 1), k("st"))
        lower = nn(data3(jnp.concatenate([s[HALF:] for s in sf], 0), 1), k("s0"))
        rest = nn(data3(jnp.concatenate(sl, 0), 1), k("s1"))
        top0 = jnp.concatenate([k("tl", 0) * sth[i] for i in range(4)], 0)
        top1 = jnp.concatenate([k("tl", l) * sth[i] for l in range(1, LEVELS) for i in range(4)], 0)
        tu = jnp.concatenate([nn(data3(top0, 1), k("s0")), nn(data3(top1, 1), k("s1"))], 0)
        full = []
        for i in range(4):
            r = tn(data3(taller(slh[i], 32), 0), k("e_tn"))
            at = HALF * i
            parts = [upper[at : at + HALF, :N], lower[at : at + HALF], upper[at : at + HALF, N:], rest[at : at + HALF]]
            t = []
            for l in range(LEVELS):
                edge = 128 * l + 8 * (8 * (i // 2) + 2 * g + i % 2)
                t.append(tu[8 * (4 * l + i) : 8 * (4 * l + i) + 8] + tu_edge[edge : edge + 8])
            t.append(zeros(88, N))
            full.append(jnp.concatenate([jnp.concatenate(parts, 0) + r] + t, 0))
        out = nn(k("o"), data3(jnp.concatenate(full, 1), 0))
        for i in range(4):
            out_ref[i // 2, 2 * g + i % 2] = lanes(out, i)


VMEM = pl.BlockSpec(memory_space=pltpu.VMEM)


def call(kernel, arguments, shapes, flops, scratch=(), in_specs=None, limit=40):
    return pl.pallas_call(
        kernel,
        in_specs=in_specs or [VMEM] * len(arguments),
        out_specs=[VMEM] * len(shapes),
        out_shape=[s if hasattr(s, "dtype") else jax.ShapeDtypeStruct(s, jnp.float32) for s in shapes],
        scratch_shapes=scratch,
        cost_estimate=pl.CostEstimate(flops=flops, bytes_accessed=1 << 20, transcendentals=0),
        compiler_params=pltpu.CompilerParams(vmem_limit_bytes=limit * 1024 * 1024),
    )(*arguments)


def exchange(value, axis, odd):
    count = lax.axis_size(axis)
    pairs = [(i, (i + 1 if i % 2 == odd else i - 1) % count) for i in range(count)]
    return lax.ppermute(value, axis, pairs)


def partner(value):
    return lax.ppermute(value, "ens", [(0, 1), (1, 0)])


def buffer(count, height):
    return pltpu.VMEM((count, height, N), jnp.float32)


def held(names):
    return [jnp.asarray(array) for array in packed(names)[0]]


def shards(x_hbm, clim_hbm):
    xp = partner(x_hbm)
    m1, m2 = (X_ROWS, N), (Y_ROWS, N)
    q = held(FIRST)[0]
    hbm = pl.BlockSpec(memory_space=pltpu.HBM)
    xa, xb, sx, x, clim = call(
        first_kernel,
        (x_hbm, clim_hbm, q),
        [m1, m1, (160, N), x_hbm.shape, clim_hbm.shape],
        10**8,
        [pltpu.VMEM(q.shape, q.dtype), pltpu.SemaphoreType.DMA((6,))],
        [hbm] * 3,
        60,
    )
    ra, rb = exchange(xa, "tx", 0), exchange(xb, "tx", 1)
    z, strips, tops, cf, cl = call(
        beside_kernel,
        (x, clim, *held(BESIDE)),
        [(IMAGES * N, 256), (IMAGES * 8, N), (32, N), (8, N, N), (8, HALF, N)],
        10**9,
    )
    ya, yb, up, fr, fl = call(
        second_kernel, (ra, rb, sx, strips, tops, *held(SECOND)), [m2, m2, m2, (160, N), (432, N)], 10**9
    )
    sa, sb = exchange(ya, "ty", 0), exchange(yb, "ty", 1)
    frp, flp, upp = partner(fr), partner(fl), partner(up)
    wf, wl, lh, clh, order = call(
        third_kernel,
        (z, xp, fr, fl, frp, flp, *held(THIRD)),
        [(2, IMAGES, N, N), (2, IMAGES, HALF, N), (2, IMAGES, EXT, 256), (8, EXT, 256), (8, N)],
        2 * 10**9,
        [buffer(32, h) for h in (136, 136, 72, 40, 24, 16)],
    )
    got = call(sort_kernel, (sa, sb, order), [(192, N)], 10**6)[0]
    gotp = partner(got)
    arguments = (wf, wl, lh, cf, cl, clh, got, gotp, up, upp, *held(FOURTH))
    return call(fourth_kernel, arguments, [x_hbm.shape], 10**9)[0]


def solution(mesh):
    in_specs = (P("ens", None, "ty", "tx"), P(None, "ty", "tx"))
    out_specs = P("ens", None, "ty", "tx")
    return jax.shard_map(shards, mesh=mesh, in_specs=in_specs, out_specs=out_specs, check_vma=False)
```

```python
import functools
import math

import jax
import jax.numpy as jnp
import ml_dtypes
import numpy as np
from jax import lax
from jax.experimental import pallas as pl
from jax.experimental.pallas import tpu as pltpu
from jax.sharding import PartitionSpec as P

LEVELS = 5
N = 128
EXT = 24

root_three = math.sqrt(3.0)
norm_factor = 4.0 * math.sqrt(2.0)
low_taps = np.array([1.0 + root_three, 3.0 + root_three, 3.0 - root_three, 1.0 - root_three]) / norm_factor
high_taps = np.array([low_taps[3], -low_taps[2], low_taps[1], -low_taps[0]])


def express(rows, basis):
    solved = np.linalg.lstsq(basis.T, rows.T, rcond=1e-9)[0].T
    assert np.abs(solved @ basis - rows).max() < 1e-10
    return solved


def build():
    approx = np.zeros((N + 2, N))
    approx[2:] = np.eye(N)
    A = np.zeros((256, N))
    PM = np.zeros((256, N))
    level = np.zeros(256, int)
    is_low = np.zeros(256, bool)
    valid = np.zeros(256, bool)
    E = np.zeros((EXT, N))
    last = np.zeros((EXT, N))
    last_pm = np.zeros((EXT, N))
    ext_level = np.full(EXT, -1)
    ext_low = np.zeros(EXT, bool)
    S = np.zeros((LEVELS, N))
    T = []
    up = np.zeros((LEVELS, 3, N))
    down = np.zeros((LEVELS, 3, N))
    up_k = np.zeros((LEVELS, 4, 3))
    down_k = np.zeros((LEVELS, 4, 3))
    where_last = np.zeros((LEVELS, 4), int)
    offset, count = 0, N
    for l in range(LEVELS):
        half = count // 2
        bands = []
        for taps in (low_taps, high_taps):
            band = np.zeros((half + 2, N))
            for k in range(-2, half):
                for j in range(4):
                    if -2 <= 2 * k + j < count:
                        band[k + 2] += taps[j] * approx[2 * k + j + 2]
            bands.append(band)
        stride = 2**l
        for b, band in enumerate(bands):
            width = max(half, 8)
            start = offset + width - half
            A[start : start + half] = band[2:]
            valid[start : start + half] = True
            level[offset : offset + width] = l
            is_low[offset : offset + width] = b == 0
            for k in range(half):
                PM[start + k, 2 * stride * k + (0 if b == 0 else stride)] = 1.0
            for k in range(2):
                e = 4 * l + 2 * b + k
                where_last[l, 2 * b + k] = start + half - 2 + k
                ext_level[e], ext_low[e] = l, b == 0
                if l > 0 or k == 1:
                    E[e] = band[k]
                    last[e] = A[start + half - 2 + k]
                    last_pm[e] = PM[start + half - 2 + k]
                else:
                    ext_level[e] = -1
            offset += width
        S[l] = low_taps[2] * approx[2] + low_taps[3] * approx[3]
        t = low_taps[0] * approx[count] + low_taps[1] * approx[count + 1]
        if l == 0:
            T.append(t)
            up[0, 0], down[0, 0] = S[0], t
        else:
            if l == 1:
                T.append(t)
            T += [bands[0][half], bands[1][half]]
            up[l] = np.stack([approx[0], approx[1], S[l]])
            down[l] = np.stack([t, bands[0][half], bands[1][half]])
        up_k[l] = express(E[4 * l : 4 * l + 4], up[l])
        down_k[l] = express(last[4 * l : 4 * l + 4], down[l])
        approx, count = bands[0], half
    T = np.stack(T)
    same = (level[:, None] == level[None, :]) & valid[:, None] & valid[None, :]
    mask = same & ~(is_low[:, None] & is_low[None, :] & (level[:, None] < 4))
    c = {}
    c["A"], c["PM"] = A, PM
    c["E"] = E
    c["S"], c["T"] = S, T
    c["KE"], c["KA"] = express(E, S), express(last, T)
    place = np.zeros((256, EXT))
    for l in range(LEVELS):
        for q in range(4):
            place[where_last[l, q], 4 * l + q] = 1.0
    c["GS"] = (place @ c["KE"]).T
    columns = sorted({int(np.argmax(r)) for r in last_pm if r.any()})
    D = np.zeros((12, N))
    for i, col in enumerate(columns):
        D[i, col] = 1.0
    c["D"] = D
    c["KD"] = last_pm @ D.T
    Y = np.zeros((LEVELS, 8, N))
    PY = np.zeros((LEVELS, 8, N))
    PYC = np.zeros((LEVELS, 8, N))
    for l in range(LEVELS):
        if l == 0:
            Y[0, 3], Y[0, 7] = up[0, 0], down[0, 0]
            PY[0, 4:8] = last_pm[0:4]
        else:
            Y[l, 0:3], Y[l, 4:7] = up[l], down[l]
            PY[l, 0:4] = last_pm[4 * l : 4 * l + 4]
        PYC[l, 0:4] = last_pm[4 * l : 4 * l + 4]
    c["Y"], c["PY"], c["PYC"] = Y.reshape(40, N), PY.reshape(40, N), PYC.reshape(40, N)
    GK = np.zeros((256, 4))
    cup = np.zeros((4, 8, N))
    cdn = np.zeros((4, 8, N))
    hup = np.zeros((4, 8, 96))
    hdn = np.zeros((4, 8, 96))
    lane_level = level[128:]
    ext96 = np.tile(ext_level, 4)
    for l in range(LEVELS):
        for q in range(4):
            for j in range(3):
                row = 3 if l == 0 else j
                if l == 0 and j > 0:
                    continue
                GK[where_last[l, q], row] = up_k[l, q, j]
                if l == 0:
                    cup[3, 4 + q, :] = up_k[0, q, 0]
                    cdn[3, 4 + q, :] = down_k[0, q, 0]
                else:
                    cup[j, q, lane_level == l] = up_k[l, q, j]
                    cdn[j, q, lane_level == l] = down_k[l, q, j]
                hup[row, q, ext96 == l] = up_k[l, q, j]
                hdn[row, q, ext96 == l] = down_k[l, q, j]
    c["GK"] = GK
    c["cup"], c["cdn"], c["hup"], c["hdn"] = cup, cdn, hup, hdn
    c["m0"], c["m1"] = mask[:128, :128], mask[128:, 128:]
    ext_mask = (ext_level[:, None] == level[None, :]) & valid[None, :]
    ext_mask &= ~(ext_low[:, None] & is_low[None, :] & (level[None, :] < 4))
    c["mlh"] = ext_mask
    mth = np.zeros((8, N), bool)
    for q in range(4):
        low = q < 2
        mth[q] = valid[128:] & ~(low & is_low[128:] & (lane_level < 4))
        if q % 2 == 1:
            mth[4 + q] = ~(low & is_low[:128])
    c["mth"] = mth
    mch = np.zeros((8, EXT), bool)
    for q in range(4):
        low = q < 2
        mch[q] = (ext_level >= 0) & ~(low & ext_low & (ext_level < 4))
        mch[q] &= ~((ext_level == 0) & (q % 2 == 0))
    c["mch"] = np.tile(mch, (1, 4))
    c["lane_level"], c["ext_level"] = lane_level, ext_level
    return c


def pad_rows(matrix, rows):
    return np.concatenate([matrix, np.zeros((rows - matrix.shape[0],) + matrix.shape[1:])], 0)


def pad_cols(matrix, cols):
    return pad_rows(matrix.T, cols).T


IMAGES = 16
HX = IMAGES * EXT
X_ROWS = 208
Y_ROWS = 112


@functools.cache
def constants():
    c = build()
    k = {}

    def parts(name, matrix, axis):
        k[name] = ("parts", axis, matrix)

    def exact(name, matrix, axis):
        k[name] = ("exact", axis, matrix)

    def mask(name, array):
        k[name] = ("mask", None, np.asarray(array, np.float64))

    def plain(name, array):
        k[name] = ("plain", None, np.asarray(array, np.float64))

    parts("q_nt", np.concatenate([pad_rows(c["T"], 16), pad_rows(c["S"], 16)]), 1)
    exact("d_nt", pad_rows(c["D"], 16), 1)
    parts("at", c["A"].T, 0)
    parts("gs", pad_rows(c["GS"], 16), 0)
    fours = np.kron(np.eye(4), np.concatenate([c["KE"], np.zeros((EXT, 5))], 1))
    parts("kz", pad_cols(np.concatenate([np.kron(np.eye(4), c["KA"]), fours], 1), 128), 1)
    exact("kd", pad_cols(np.kron(np.eye(4), c["KD"]), 128), 1)
    parts("y_nt", pad_rows(c["Y"], 48), 1)
    exact("pt", c["PM"].T, 0)
    exact("p0", c["PM"][:128], 1)
    exact("p1", c["PM"][128:], 1)
    exact("py", pad_rows(c["PY"], 48), 1)
    exact("pyc_nt", pad_rows(c["PYC"], 48), 1)
    gst = np.zeros((128, 256))
    for i in range(8):
        gst[10 * i : 10 * i + 5] = c["GS"]
    parts("gst", gst, 0)
    kdb = np.zeros((128, 128))
    for i in range(4):
        kdb[12 * i : 12 * i + 12, EXT * i : EXT * (i + 1)] = c["KD"].T
    exact("kdb", kdb, 0)
    own = np.zeros((8, 8, 128))
    for i in range(8):
        own[i, :, 10 * i : 10 * i + 10] = 1.0
    mask("own", own)
    parts("gkt", pad_cols(c["GK"], 16).T, 0)
    left = np.arange(N) < 64
    w = np.zeros((9, 4, 8, N))
    for j in range(4):
        g = c["GK"][:, j : j + 1]
        w[0, j] = np.where(left, g[152:160], 0)
        w[1, j] = np.where(left, g[184:192], g[56:64])
        w[2, j] = g[120:128]
        for n, start in enumerate((200, 216, 224, 232, 240, 248)):
            w[3 + n, j] = g[start : start + 8]
    assert np.isclose(np.abs(w[..., 0]).sum() + np.abs(c["GK"][56:64]).sum(), np.abs(c["GK"]).sum())
    plain("gkc", w)
    top = np.concatenate([np.where(left[:, None], 0, c["A"][:N]), np.where(left[:, None], c["A"][N:], 0)], 1)
    parts("st", top, 0)
    parts("s0", c["A"][:128], 0)
    parts("s1", c["A"][128:], 0)
    upper = np.where(left, c["m1"][:64], c["m0"][:64])
    mask("mf", np.concatenate([upper, c["m0"][64:]]))
    mask("ml", c["m1"][64:])
    parts("e_tn", pad_rows(c["E"], 32), 0)
    plain("cup", c["cup"])
    plain("cdn", c["cdn"])
    plain("hup", np.tile(c["hup"][:, :, :EXT], (1, 1, IMAGES)))
    plain("hdn", np.tile(c["hdn"][:, :, :EXT], (1, 1, IMAGES)))
    lane = c["lane_level"]
    ext = np.tile(c["ext_level"], IMAGES)
    mask("fold", np.stack([np.broadcast_to(lane == l, (8, N)) for l in range(1, LEVELS)]))
    mask("foldx", np.stack([np.broadcast_to(ext == l, (8, HX)) for l in range(LEVELS)]))
    mask("mlh", c["mlh"])
    mask("mth", c["mth"])
    mask("mch", np.tile(c["mch"][:, :EXT], (1, 8)))
    tl = np.zeros((LEVELS, 8, N))
    tl[0, 4:8] = 1.0
    for l in range(1, LEVELS):
        tl[l, 0:4, lane == l] = 1.0
    mask("tl", tl)
    cl = np.zeros((LEVELS, 8, 3, 32))
    for l in range(LEVELS):
        cl[l, slice(4, 8) if l == 0 else slice(0, 4), :, :EXT] = c["ext_level"] == l
    mask("cl", cl.reshape(LEVELS, 8, 96))
    return k


def pieces(array, tile):
    array = array.reshape((-1,) + array.shape[-2:])
    width = -(-array.shape[2] // N) * N
    height = -(-array.shape[1] // tile) * tile
    full = np.zeros((array.shape[0], height, width))
    full[:, : array.shape[1], : array.shape[2]] = array
    return full.reshape(array.shape[0], height, width // N, N).transpose(0, 2, 1, 3)


@functools.cache
def packed(names):
    narrow, wide, places = [np.zeros((0, N))], [np.zeros((0, N))], {}
    for name in names:
        kind, axis, array = constants()[name]
        into = wide if kind == "plain" else narrow
        blocks = pieces(array, 8 if kind == "plain" else 16)
        places[name] = (kind, axis, sum(g.shape[0] for g in into), blocks.shape, array.shape)
        if kind == "parts":
            high = blocks.astype(ml_dtypes.bfloat16).astype(np.float64)
            into += [high.reshape(-1, N), (blocks - high).reshape(-1, N)]
        else:
            into.append(blocks.reshape(-1, N))
    arrays = [np.concatenate(narrow).astype(ml_dtypes.bfloat16)]
    if len(wide) > 1:
        arrays.append(np.concatenate(wide).astype(np.float32))
    return arrays, places


def reader(names, refs):
    places = packed(names)[1]

    def read(name, *index):
        kind, axis, start, blocks, shape = places[name]
        ref = refs[1] if kind == "plain" else refs[0]
        count, columns, height, _ = blocks
        at = 0
        for dim, value in zip(shape, index):
            at = at * dim + value
        assert np.prod(shape[: len(index)], dtype=int) == count

        def one(base):
            first = [base + (at * columns + j) * height for j in range(columns)]
            block = jnp.concatenate([ref[f : f + height, :] for f in first], 1)
            return block

        if kind == "parts":
            high, low = one(start), one(start + count * columns * height)
            return jnp.concatenate([high, high, low], axis)
        if kind == "exact":
            return jnp.concatenate([one(start)] * 2, axis)
        return one(start).astype(jnp.float32)[: shape[-2], : shape[-1]]

    return read


def split(x):
    high = x.astype(jnp.bfloat16).astype(jnp.float32)
    return high, x - high


def data3(x, axis):
    high, low = split(x)
    return jnp.concatenate([high, low, high], axis).astype(jnp.bfloat16)


def data2(x, axis):
    high, low = split(x)
    return jnp.concatenate([high, low], axis).astype(jnp.bfloat16)


def nn(a, b):
    return lax.dot_general(a, b, (((1,), (0,)), ((), ())), preferred_element_type=jnp.float32)


def nt(a, b):
    return lax.dot_general(a, b, (((1,), (1,)), ((), ())), preferred_element_type=jnp.float32)


def tn(a, b):
    return lax.dot_general(a, b, (((0,), (0,)), ((), ())), preferred_element_type=jnp.float32)


def lanes(x, i):
    return x[:, N * i : N * (i + 1)]


def rows(x, i):
    return x[N * i : N * (i + 1)]


def side_by_side(x):
    return jnp.concatenate([rows(x, i) for i in range(x.shape[0] // N)], 1)


def zeros(*shape):
    return jnp.zeros(shape, jnp.float32)


def wider(x, width):
    return jnp.concatenate([x, zeros(x.shape[0], width - x.shape[1])], 1)


def taller(x, height):
    return jnp.concatenate([x, zeros(height - x.shape[0], x.shape[1])], 0)


def even_place(axis):
    return lax.axis_index(axis) % 2 == 0


HALF = 64
H = [float(t) for t in low_taps]
G = [float(t) for t in high_taps]


FIRST = ("q_nt", "d_nt")


def first_kernel(x_hbm, clim_hbm, q_hbm, a_ref, b_ref, s_ref, x_ref, clim_ref, q_ref, sems):
    even = even_place("tx")
    ens = lax.axis_index("ens")
    pairs = [(q_hbm.at[pl.ds(0, q_ref.shape[0])], q_ref)]
    for m in range(2):
        for h in range(2):
            pairs.append((x_hbm.at[m, pl.ds(4 * h, 4)], x_ref.at[m, pl.ds(4 * h, 4)]))
    pairs.append((clim_hbm.at[pl.ds(4 * ens, 4)], clim_ref))
    copies = [pltpu.make_async_copy(src, dst, sems.at[i]) for i, (src, dst) in enumerate(pairs)]
    for copy in copies:
        copy.start()
    copies[0].wait()
    k = reader(FIRST, (q_ref,))
    q = k("q_nt")
    right, left = [], []
    for g in range(4):
        copies[1 + g].wait()
        x3 = data3(x_ref[g // 2, 4 * (g % 2) : 4 * (g % 2) + 4].reshape(4 * N, N), 1)
        u = nt(q, x3)
        right += [lanes(u, i)[0:10] for i in range(4)]
        left += [lanes(u, i)[16:26] for i in range(4)]
    copies[5].wait()
    d = nt(k("d_nt"), data2(clim_ref[...].reshape(4 * N, N), 1))
    right += [lanes(d, j)[0:12] for j in range(4)]
    left = jnp.concatenate(left, 0)
    s_ref[...] = left
    right, left = jnp.concatenate(right, 0), taller(left, X_ROWS)
    a_ref[...] = jnp.where(even, right, left)
    b_ref[...] = jnp.where(even, left, right)


def order_kernel(x_ref, out_ref):
    out_ref[...] = x_ref[0:8]


BESIDE = (
    "at", "fold", "foldx", "gst", "kdb", "kz", "mf", "ml", "own", "p0", "p1", "pt", "py", "pyc_nt",
    "y_nt",
)


def beside_kernel(x_ref, xp_ref, clim_ref, order_ref, *refs):
    n = len(packed(BESIDE)[0])
    k = reader(BESIDE, refs[:n])
    z_ref, zp_ref, s_ref, c_ref, cf_ref, cl_ref = refs[n:]
    ens = lax.axis_index("ens")
    at = k("at")
    for g in range(4):
        x = x_ref[g // 2, 4 * (g % 2) : 4 * (g % 2) + 4].reshape(4 * N, N)
        z_ref[4 * N * g : 4 * N * (g + 1), :] = nn(data3(x, 1), at)
        y = nn(k("y_nt"), data3(side_by_side(x), 0))
        y = jnp.concatenate([lanes(y, i)[0:40] for i in range(4)], 0)
        y = nn(data3(y, 1), at)
        for i in range(4):
            strip = y[40 * i : 40 * i + 8, :N]
            for l in range(4):
                strip = strip + k("fold", l) * y[40 * i + 8 * l + 8 : 40 * i + 8 * l + 16, N:]
            s_ref[8 * (4 * g + i) : 8 * (4 * g + i) + 8, :] = strip
    for g in range(4):
        x = xp_ref[g // 2, 4 * (g % 2) : 4 * (g % 2) + 4].reshape(4 * N, N)
        zp_ref[4 * N * g : 4 * N * (g + 1), :] = nn(data3(x, 1), at)
    clim = clim_ref[pl.ds(4 * ens, 4)].reshape(4 * N, N)
    y = nn(k("py"), data2(side_by_side(clim), 0))
    y = jnp.concatenate([lanes(y, i)[0:40] for i in range(4)], 0)
    y = nn(data2(y, 1), k("pt"))
    for i in range(4):
        strip = y[40 * i : 40 * i + 8, :N]
        for l in range(4):
            strip = strip + k("fold", l) * y[40 * i + 8 * l + 8 : 40 * i + 8 * l + 16, N:]
        c_ref[8 * i : 8 * i + 8, :] = strip
    inside = lax.broadcasted_iota(jnp.int32, (HALF, N), 1) < HALF
    for g in range(2):
        cz = nn(data2(clim_ref[4 * g : 4 * g + 4].reshape(4 * N, N), 1), k("pt"))
        c0 = nn(k("p0"), data2(side_by_side(cz[:, :N]), 0))
        c1 = nn(k("p1"), data2(side_by_side(cz[:, N:]), 0))
        for j in range(4):
            w0, w1 = lanes(c0, j), lanes(c1, j)
            upper = jnp.where(inside, w1[:HALF], w0[:HALF])
            cf_ref[4 * g + j] = 0.5 * k("mf") * jnp.concatenate([upper, w0[HALF:]], 0)
            cl_ref[4 * g + j] = 0.5 * k("ml") * w1[HALF:]


SECOND = (
    "fold", "foldx", "gst", "kdb", "kz", "own", "pyc_nt", "y_nt",
)


def second_kernel(ra_ref, rb_ref, sx_ref, s_ref, c_ref, *refs):
    n = len(packed(SECOND)[0])
    k = reader(SECOND, refs[:n])
    a_ref, b_ref, share_ref = refs[n:]
    kz = k("kz")
    even, even_y = even_place("tx"), even_place("ty")
    ra, rb = ra_ref[...], rb_ref[...]
    from_right, from_left = jnp.where(even, ra[:160], rb[:160]), jnp.where(even, rb, ra)
    share_ref[432:592] = from_right
    strips = []
    for g in range(2):
        f = taller(from_right[80 * g : 80 * g + 80], 128)
        y = nt(k("y_nt"), data3(f, 1))[0:40]
        spread = jnp.concatenate(
            [k("own", i) * y[8 * l : 8 * l + 8] for i in range(8) for l in range(LEVELS)], 0
        )
        t = nn(data3(spread, 1), k("gst"))
        for i in range(8):
            at = 40 * i
            strip = s_ref[64 * g + 8 * i : 64 * g + 8 * i + 8, :] + t[at : at + 8, :N]
            for l in range(4):
                strip = strip + k("fold", l) * t[at + 8 * l + 8 : at + 8 * l + 16, N:]
            strips.append(strip)
    for g in range(4):
        f = jnp.concatenate([from_left[40 * g : 40 * g + 40], sx_ref[40 * g : 40 * g + 40]], 0)
        share_ref[96 * g : 96 * g + 96] = nn(kz, data3(taller(f, 128), 0))
    share_ref[384:432] = from_left[160:208]
    hy = nt(k("y_nt"), data3(share_ref[0:384], 1))
    corner = sum(k("foldx", l) * hy[8 * l : 8 * l + 8] for l in range(LEVELS))
    cx = nt(k("pyc_nt"), data2(taller(from_left[160:208], 128), 1))[0:40]
    cc = nn(data2(cx, 1), k("kdb"))
    cc = sum(k("foldx", l)[:, :N] * cc[8 * l : 8 * l + 8] for l in range(LEVELS))
    up = [s[0:4] for s in strips] + [lanes(corner, g)[0:4] for g in range(3)] + [zeros(36, N)]
    down = [s[4:8] for s in strips] + [lanes(corner, g)[4:8] for g in range(3)] + [cc[0:4], c_ref[...]]
    up, down = jnp.concatenate(up, 0), jnp.concatenate(down, 0)
    a_ref[...] = jnp.where(even_y, down, up)
    b_ref[...] = jnp.where(even_y, up, down)
    share_ref[592:704] = up


def filtered(ref, count):
    parts = [ref[pl.ds(j, count, stride=2), :] for j in range(4)]
    low = H[0] * parts[0] + H[1] * parts[1] + H[2] * parts[2] + H[3] * parts[3]
    high = G[0] * parts[0] + G[1] * parts[1] + G[2] * parts[2] + G[3] * parts[3]
    return low, high


THIRD = (
    "at", "gs", "kd", "mlh", "pt",
)


def third_kernel(z_ref, zp_ref, share_ref, sharep_ref, *refs):
    n = len(packed(THIRD)[0])
    k = reader(THIRD, refs[:n])
    wf_ref, wl_ref, lh_ref, clh_ref, order_ref = refs[n : n + 5]
    z0_buf, z1_buf, a_buf, b_buf, c_buf, d_buf = refs[n + 5 :]
    first = lax.axis_index("ens") == 0
    inside = lax.broadcasted_iota(jnp.int32, (HALF, N), 1) < HALF
    at = k("at")
    def group(g, side, z_from, share):
        f = [share[pl.ds(432 + 40 * g + 8 * i, 8), :] for i in range(5)]
        f = jnp.concatenate(f, 0)
        f = jnp.concatenate([f[10 * i : 10 * i + 5] for i in range(4)], 1)
        z = tn(data3(taller(f, 16), 0), k("gs"))
        z = z + z_from[pl.ds(4 * N * g, 4 * N), :]
        zl = share[pl.ds(96 * g, 96), :]
        lh_ref[side, pl.ds(4 * g, 4)] = nn(data3(zl, 1), at).reshape(4, EXT, 256)
        for i in range(4):
            image = 4 * g + i
            slot = 16 * side + image
            z0_buf[slot, 0:N] = rows(z, i)[:, :N]
            z1_buf[slot, 0:N] = rows(z, i)[:, N:]
            z0_buf[slot, N : N + 8] = zeros(8, N)
            z1_buf[slot, N : N + 8] = zeros(8, N)
            low0, high0 = filtered(z0_buf.at[slot], 64)
            a_buf[slot, 0:64] = filtered(z1_buf.at[slot], 64)[0]
            a_buf[slot, 64:72] = zeros(8, N)
            low1, high1 = filtered(a_buf.at[slot], 32)
            b_buf[slot, 0:32] = low1
            b_buf[slot, 32:40] = zeros(8, N)
            low2, high2 = filtered(b_buf.at[slot], 16)
            c_buf[slot, 0:16] = low2
            c_buf[slot, 16:24] = zeros(8, N)
            low3, high3 = filtered(c_buf.at[slot], 8)
            d_buf[slot, 0:8] = low3
            d_buf[slot, 8:16] = zeros(8, N)
            low4, high4 = filtered(d_buf.at[slot], 4)
            wf_ref[side, image, 0:64] = jnp.where(inside, jnp.concatenate([low1, high1], 0), low0)
            wf_ref[side, image, 64:128] = high0
            wl_ref[side, image] = jnp.concatenate(
                [low2, high2, low3, high3, zeros(4, N), low4, zeros(4, N), high4], 0
            )

    for g in range(4):
        group(g, 0, z_ref, share_ref)
        group(g, 1, zp_ref, sharep_ref)
    mine, other = share_ref[384:432], sharep_ref[384:432]
    halos = [jnp.where(first, mine, other), jnp.where(first, other, mine)]
    for g in range(2):
        cl = nn(k("kd"), data2(taller(halos[g], 128), 0))
        clh = nn(data2(cl, 1), k("pt"))
        for j in range(4):
            clh_ref[4 * g + j] = 0.5 * k("mlh") * clh[EXT * j : EXT * (j + 1)]
    order_ref[...] = zeros(8, N)


def sort_kernel(sa_ref, sb_ref, order_ref, out_ref):
    even_y = even_place("ty")
    a, b = sa_ref[...], sb_ref[...]
    out_ref[0:80] = jnp.where(even_y, a, b)[0:80]
    out_ref[80:192] = jnp.where(even_y, b, a)


FOURTH = (
    "cdn", "cl", "cup", "e_tn", "gkc", "gkt", "hdn", "hup", "mch", "mf", "ml", "mlh", "mth", "s0",
    "s1", "st", "tl",
)


def fourth_kernel(wf_ref, wl_ref, lh_ref, cf_ref, cl_ref, clh_ref, got_ref, gotp_ref, share_ref, sharep_ref, *refs):
    n = len(packed(FOURTH)[0])
    k = reader(FOURTH, refs[:n])
    out_hbm, out_ref, sems, *bufs = refs[n:]
    copies = []
    first = lax.axis_index("ens") == 0
    belows, aboves, ups, lhs, chs = [], [], [], [], []
    for got, share in ((got_ref, share_ref), (gotp_ref, sharep_ref)):
        below, above, up = got[0:80], got[80:192], share[592:704]
        hb = jnp.concatenate([below[64 + 4 * g : 68 + 4 * g] for g in range(3)], 1)
        lhs.append(tn(data3(taller(hb, 16), 0), k("gkt")))
        hu = jnp.concatenate([up[64 + 4 * g : 68 + 4 * g] for g in range(3)], 1)
        hd = jnp.concatenate([above[64 + 4 * g : 68 + 4 * g] for g in range(3)], 1)
        ch = zeros(8, HX)
        for j in range(4):
            ch = ch + k("hup", j) * hu[j : j + 1] + k("hdn", j) * hd[j : j + 1]
        belows.append(below)
        aboves.append(above)
        ups.append(up)
        chs.append(ch)
    halos = [jnp.where(first, aboves[0], aboves[1])[76:112], jnp.where(first, aboves[1], aboves[0])[76:112]]

    def top(side, i):
        t = zeros(8, N)
        for j in range(4):
            at = 4 * i + j
            t = t + k("cup", j) * ups[side][at : at + 1] + k("cdn", j) * aboves[side][at : at + 1]
        return t

    def grown(w, side, i, groups):
        parts, done = [], 0
        for start, which, js in groups:
            if start > done:
                parts.append(w[done:start])
            part = w[start : start + 8]
            for j in js:
                part = part + k("gkc", which, j) * belows[side][4 * i + j : 4 * i + j + 1]
            parts.append(part)
            done = start + 8
        return jnp.concatenate(parts + ([w[done:]] if done < w.shape[0] else []), 0)

    def variance(half_clim, mask, parts):
        total = parts[0] * parts[0]
        for part in parts[1:]:
            total = total + part * part
        return half_clim + (0.125 * mask) * total

    in_full = ((24, 0, (0, 1, 2)), (56, 1, (0, 1, 2, 3)), (120, 2, (3,)))
    in_rest = tuple((start, 3 + n, (0, 1, 2)) for n, start in enumerate((8, 24, 32, 40, 48, 56)))
    cch = jnp.concatenate([h[0:4, 0:96] for h in halos], 1)
    cch = jnp.concatenate([cch, zeros(4, 192)], 0)
    vch = variance(0.5 * k("mch") * cch, k("mch"), [c[:, 192 * m : 192 * m + 192] for c in chs for m in range(2)])
    sch = [chs[0][:, 192 * m : 192 * m + 192] * vch for m in range(2)]
    sch = [wider(s, 256) for s in sch]
    edge = []
    for i in range(IMAGES):
        at = EXT * (i % 8)
        c = sch[i // 8][0:4, at : at + EXT]
        edge.append(jnp.concatenate([c, c], 0))
    high, low = split(wider(jnp.concatenate(edge, 0), 32))
    edge = jnp.concatenate([high, low, high], 1)
    edge = jnp.concatenate([k("cl", l) * edge[8 * i : 8 * i + 8] for l in range(LEVELS) for i in range(IMAGES)], 0)
    tu_edge = nn(edge.astype(jnp.bfloat16), k("e_tn"))
    for g in range(4):
        sf, sl, slh, sth = [None] * 4, [None] * 4, [None] * 4, [None] * 4
        for n in range(2):
            v = 2 * g + n
            four = [(side, v + 8 * m) for side in range(2) for m in range(2)]
            wf = [grown(wf_ref[side, i], side, i, in_full) for side, i in four]
            wl = [grown(wl_ref[side, i], side, i, in_rest) for side, i in four]
            lh = [lh_ref[side, i] + lhs[side][EXT * i : EXT * (i + 1)] for side, i in four]
            th = [top(side, i) for side, i in four]
            vf = variance(cf_ref[v], k("mf"), wf)
            vl = variance(cl_ref[v], k("ml"), wl)
            vlh = variance(clh_ref[v], k("mlh"), lh)
            climth = halos[v // 4][4 + 8 * (v % 4) : 12 + 8 * (v % 4)]
            vth = variance(0.5 * k("mth") * climth, k("mth"), th)
            for m in range(2):
                sf[2 * m + n] = wf[m] * vf
                sl[2 * m + n] = wl[m] * vl
                slh[2 * m + n] = lh[m] * vlh
                sth[2 * m + n] = th[m] * vth
        upper = nn(data3(jnp.concatenate([s[:HALF] for s in sf], 0), 1), k("st"))
        lower = nn(data3(jnp.concatenate([s[HALF:] for s in sf], 0), 1), k("s0"))
        rest = nn(data3(jnp.concatenate(sl, 0), 1), k("s1"))
        top0 = jnp.concatenate([k("tl", 0) * sth[i] for i in range(4)], 0)
        top1 = jnp.concatenate([k("tl", l) * sth[i] for l in range(1, LEVELS) for i in range(4)], 0)
        tu = jnp.concatenate([nn(data3(top0, 1), k("s0")), nn(data3(top1, 1), k("s1"))], 0)
        for i in range(4):
            m, v = i // 2, 2 * g + i % 2
            image = 8 * m + v
            r = tn(data3(taller(slh[i], 32), 0), k("e_tn"))
            at = HALF * i
            one = upper[at : at + HALF, N:] + r[N : N + HALF]
            more = rest[at : at + HALF] + r[N + HALF :]
            bands = [
                (upper[at : at + HALF, :N] + r[:HALF], lower[at : at + HALF] + r[HALF:N]),
                (one[0:32], one[32:64]),
                (more[0:16], more[16:32]),
                (more[32:40], more[40:48]),
                (more[52:56], more[60:64]),
            ]
            for l, (low, high) in enumerate(bands):
                at = 128 * l + 8 * image
                t = tu[8 * (4 * l + i) : 8 * (4 * l + i) + 8] + tu_edge[at : at + 8]
                t = t[4:8] if l == 0 else t[0:4]
                buf = bufs[l]
                buf[2 * image, 14:16] = t[0:2]
                buf[2 * image + 1, 14:16] = t[2:4]
                buf[2 * image, 16 : 16 + low.shape[0]] = low
                buf[2 * image + 1, 16 : 16 + low.shape[0]] = high
            for l in reversed(range(LEVELS)):
                count = HALF >> l
                first_row = 16 if l == 0 else 8
                size = 16 + count - first_row
                here = [bufs[l][2 * image + b, first_row : first_row + size] for b in range(2)]
                prior = [bufs[l][2 * image + b, first_row - 1 : first_row - 1 + size] for b in range(2)]
                pair = [
                    H[j] * here[0] + G[j] * here[1] + H[j + 2] * prior[0] + G[j + 2] * prior[1] for j in range(2)
                ]
                for j in range(2):
                    if l == 0:
                        out_ref[m, v, pl.ds(j, size, stride=2), :] = pair[j]
                    else:
                        place = pl.ds(j, size, stride=2)
                        bufs[l - 1][2 * image, place, :] = bufs[l - 1][2 * image, place, :] + pair[j]
        for m in range(2):
            part = pl.ds(2 * g, 2)
            copy = pltpu.make_async_copy(out_ref.at[m, part], out_hbm.at[m, part], sems.at[2 * g + m])
            copy.start()
            copies.append(copy)
    for copy in copies:
        copy.wait()


VMEM = pl.BlockSpec(memory_space=pltpu.VMEM)
HBM = pl.BlockSpec(memory_space=pltpu.HBM)


def call(kernel, arguments, shapes, flops, scratch=(), in_specs=None, limit=40, out_specs=None):
    return pl.pallas_call(
        kernel,
        in_specs=in_specs or [VMEM] * len(arguments),
        out_specs=out_specs or [VMEM] * len(shapes),
        out_shape=[s if hasattr(s, "dtype") else jax.ShapeDtypeStruct(s, jnp.float32) for s in shapes],
        scratch_shapes=scratch,
        cost_estimate=pl.CostEstimate(flops=flops, bytes_accessed=1 << 20, transcendentals=0),
        compiler_params=pltpu.CompilerParams(vmem_limit_bytes=int(limit * 1024 * 1024)),
    )(*arguments)


def exchange(value, axis, odd):
    count = lax.axis_size(axis)
    pairs = [(i, (i + 1 if i % 2 == odd else i - 1) % count) for i in range(count)]
    return lax.ppermute(value, axis, pairs)


def partner(value):
    return lax.ppermute(value, "ens", [(0, 1), (1, 0)])


def buffer(count, height):
    return pltpu.VMEM((count, height, N), jnp.float32)


PAD = True


def held(names):
    return [jnp.asarray(array) for array in packed(names)[0]]


def shards(x, clim):
    xp = partner(x)
    m1, m2 = (X_ROWS, N), (Y_ROWS, N)
    q = held(FIRST)[0]
    padded = jnp.concatenate([q, jnp.zeros((4096 - q.shape[0], N), q.dtype)], 0) if PAD else q
    scratch = [pltpu.VMEM(x.shape, x.dtype), pltpu.VMEM((4, N, N), x.dtype)]
    scratch += [pltpu.VMEM(q.shape, q.dtype), pltpu.SemaphoreType.DMA((6,))]
    xa, xb, sx = call(first_kernel, (x, clim, padded), [m1, m1, (160, N)], 10**8, scratch, [HBM] * 3, 53.6)
    ra, rb = exchange(xa, "tx", 0), exchange(xb, "tx", 1)
    order = call(order_kernel, (sx,), [(8, N)], 10**6)[0]
    z, zp, strips, tops, cf, cl = call(
        beside_kernel,
        (x, xp, clim, order, *held(BESIDE)),
        [(IMAGES * N, 256), (IMAGES * N, 256), (IMAGES * 8, N), (32, N), (8, N, N), (8, HALF, N)],
        10**9,
    )
    ya, yb, share = call(second_kernel, (ra, rb, sx, strips, tops, *held(SECOND)), [m2, m2, (704, N)], 10**9)
    sa, sb = exchange(ya, "ty", 0), exchange(yb, "ty", 1)
    sharep = partner(share)
    wf, wl, lh, clh, order = call(
        third_kernel,
        (z, zp, share, sharep, *held(THIRD)),
        [(2, IMAGES, N, N), (2, IMAGES, HALF, N), (2, IMAGES, EXT, 256), (8, EXT, 256), (8, N)],
        2 * 10**9,
        [buffer(32, h) for h in (136, 136, 72, 40, 24, 16)],
    )
    got = call(sort_kernel, (sa, sb, order), [(192, N)], 10**6)[0]
    gotp = partner(got)
    arguments = (wf, wl, lh, cf, cl, clh, got, gotp, share, sharep, *held(FOURTH))
    scratch = [pltpu.VMEM(x.shape, x.dtype), pltpu.SemaphoreType.DMA((8,))]
    scratch += [buffer(32, 16 + (HALF >> l)) for l in range(LEVELS)]
    return call(fourth_kernel, arguments, [x.shape], 10**9, scratch, out_specs=[HBM])[0]


def solution(mesh):
    in_specs = (P("ens", None, "ty", "tx"), P(None, "ty", "tx"))
    out_specs = P("ens", None, "ty", "tx")
    return jax.shard_map(shards, mesh=mesh, in_specs=in_specs, out_specs=out_specs, check_vma=False)
```
